128 devices in a mesh: chan: 16 (over y, z), pair: 8 (over x, core).
Axes of the slice: x: 4, y: 4, z: 4, core: 2. Of those that a mesh axis runs over, the one named last changes fastest.
Arguments:
- eta_blocks: bfloat16 [16, 2048, 2048], P('chan', 'pair'), may hold values from -6 to 6
- omega_blocks: bfloat16 [16, 2048, 2048], P('chan', 'pair'), may hold values from -0.125 to 0.125
- recouple: bfloat16 [16, 2048, 2048], P('chan'), may hold values from -0.125 to 0.125
- block_states: int32 [16], P('chan'), may hold values from 256 to 2048, as said below
- cross_map: int32 [16, 8], P('chan'), may hold values from 0 to 15, all different within a row
- cross_coef: float32 [16, 8], P('chan'), may hold values from -1 to 1
Outputs:
- pair_comm: bfloat16 [16, 2048, 2048], P('chan', 'pair')
- cross_comm: bfloat16 [16, 2048, 2048], P('chan', 'pair')
The draws below stay inside these ranges and needn't reach their ends.
Inputs may be any that keep to these rules, and one draw needn't show every extreme that they name: `block_states`: each channel has 256 to 2048 live states; channel 0 has all 2048 states live.
All inputs are finite; a program needn't handle non-finite values.
Results may differ from the reference program's by a relative error of at most 0.014.
Values may be sent and summed in bfloat16 or wider, within the bound.
A program may use at most 192 MiB of HBM per device.

```python
import jax
import jax.numpy as jnp
from jax import lax

B = 2048
CH_DEV = 1
NCH = 16
FAN = 8
N_CHAN = 16


def draw_block_states(key, part):
    key = jax.random.fold_in(key, 7)
    drawn = jax.random.randint(key, (NCH,), B // 8, B + 1)
    return jnp.where(jnp.arange(NCH) == 0, B, drawn).astype(jnp.int32)


def block_levels(own_key, dims, cuts, least, top_value):
    gain, own = 1.0, jax.random.fold_in(own_key, 6)
    for dim, shards_of in cuts:
        steps = jnp.exp(jax.random.uniform(jax.random.fold_in(own, dim), (shards_of,), jnp.float32, least / len(cuts), top_value / len(cuts)))
        gain = gain * jnp.repeat(steps, dims[dim] // shards_of).reshape([-1 if axis == dim else 1 for axis in range(len(dims))])
    return gain


def choose_distinct(rng, rows, number_of, top, lift):
    ranking = jax.random.permutation(jax.random.fold_in(rng, 1), number_of)
    favour = ranking
    for power in range(3):
        favour = favour * favour // number_of
    favour = favour * lift // number_of
    tickets = jax.random.randint(jax.random.fold_in(rng, 2), (rows, number_of), 0, 4096) + favour
    sure = jax.random.permutation(jax.random.fold_in(rng, 3), rows)[jnp.arange(number_of) % rows]
    tickets = jnp.where(jnp.arange(rows)[:, None] == sure[None, :], 1 << 14, tickets)
    priority = tickets * number_of + jnp.arange(number_of)
    return lax.top_k(priority.astype(jnp.int32), top)[1].astype(jnp.int32)


def normal_values(rng, dims, width, bound, split=(), held_as=jnp.bfloat16):
    values = width * jax.random.normal(rng, dims, jnp.float32)
    if split:
        values = values * block_levels(rng, dims, split, -0.22, 0.18)
    return jnp.clip(values, -bound, bound).astype(held_as)


def setup_inputs(seed: int = 0) -> dict:
    seeds = jax.random.split(jax.random.key(seed), 7)
    eta_blocks = normal_values(seeds[0], (NCH, B, B), 1.0, 6.0, ((0, 16), (1, 8)))
    omega_blocks = normal_values(seeds[1], (NCH, B, B), B ** -0.5, 0.125, ((0, 16), (1, 8)))
    recouple = normal_values(seeds[2], (NCH, B, B), B ** -0.5, 0.125, ((0, 16),))
    block_states = draw_block_states(jax.random.fold_in(seeds[6], 71), 0)
    cross_map = choose_distinct(seeds[4], NCH, NCH, FAN, 0)
    cross_coef = jnp.clip(jax.random.uniform(seeds[5], (NCH, FAN), jnp.float32, -1.0, 1.0) * block_levels(seeds[5], (NCH, FAN), ((0, 16),), -0.4, 0.0), -1.0, 1.0)
    return dict(eta_blocks=eta_blocks, omega_blocks=omega_blocks, recouple=recouple, block_states=block_states, cross_map=cross_map, cross_coef=cross_coef)


def reference(eta_blocks, omega_blocks, recouple, block_states, cross_map, cross_coef):
    positions = jnp.arange(B, dtype=jnp.int32)
    weighing = jnp.sum(cross_coef[:, :, None] * (cross_map[:, :, None] == jnp.arange(NCH, dtype=jnp.int32)[None, None, :]).astype(jnp.float32), axis=1)

    def channel_step(chan_index):
        limit = block_states[chan_index]
        live = (positions[:, None] < limit) & (positions[None, :] < limit)
        eta_m = jnp.where(live, eta_blocks[chan_index], jnp.zeros((), jnp.bfloat16))
        omega_m = jnp.where(live, omega_blocks[chan_index], jnp.zeros((), jnp.bfloat16))
        pair_part = jnp.dot(eta_m, omega_m, preferred_element_type=jnp.float32) - jnp.dot(omega_m, eta_m, preferred_element_type=jnp.float32)
        eta_cross = jnp.dot(eta_m, recouple[chan_index], preferred_element_type=jnp.float32).astype(jnp.bfloat16)
        omega_cross = jnp.dot(omega_m, recouple[chan_index], preferred_element_type=jnp.float32).astype(jnp.bfloat16)
        product = lax.dot_general(eta_cross, omega_cross, (((1,), (1,)), ((), ())), preferred_element_type=jnp.float32)
        return pair_part.astype(jnp.bfloat16), product

    pair_comm, products = lax.map(channel_step, jnp.arange(NCH, dtype=jnp.int32))
    grouped = products.reshape(N_CHAN, CH_DEV, B, B)
    group_weights = weighing.reshape(N_CHAN, CH_DEV, NCH)

    def cross_step(target):
        factor = group_weights[:, :, target]
        partial_value = jnp.sum(factor[:, :, None, None] * grouped, axis=1)
        rounded = lax.optimization_barrier(partial_value.astype(jnp.bfloat16))
        return jnp.sum(rounded.astype(jnp.float32), axis=0).astype(jnp.bfloat16)

    cross_comm = lax.map(cross_step, jnp.arange(NCH, dtype=jnp.int32))
    return pair_comm, cross_comm
```

```python
import functools

import jax
import jax.numpy as jnp
from jax import lax
from jax.experimental import pallas as pl
from jax.experimental.pallas import tpu as pltpu
from jax.sharding import PartitionSpec as P

MESH = pl.DeviceIdType.MESH
BF = jnp.bfloat16
F32 = jnp.float32
NN = (((1,), (0,)), ((), ()))
NT = (((1,), (1,)), ((), ()))
SIDE = 4
PIECES = 4
COPIES = 128


def dot(a, b, dims):
    return lax.dot_general(a, b, dims, preferred_element_type=F32)


def kernel(
    states_ref, map_ref, coef_ref, eta_hbm, omega_hbm, rec_hbm, pair_hbm, cross_hbm,
    om, eta_half, eta_left, om_left, eta_near, rec, e_ref, f_ref,
    gath, own_sum, sum_next, sum_prev, sum_two, merge, fin_a, fin_b,
    acc, pair_out, pair_send, cross_out, wrow, wvec,
    ssem, rsem, lsem,
):
    rows, width = eta_hbm.shape
    half = width // 2
    quarter = rows
    sub = rows // PIECES
    ch, pr = lax.axis_index("chan"), lax.axis_index("pair")
    y, z, x, c = ch // SIDE, ch % SIDE, pr // 2, pr % 2
    dn = 1 - 2 * ((x + c) % 2)
    xn, xf, xo = (x + dn + SIDE) % SIDE, (x - dn + SIDE) % SIDE, (x + 2) % SIDE
    turn = 1 - 2 * c
    h = x % 2
    hf = 1 - h
    near, far, sib = (ch, xn * 2 + c), (ch, xf * 2 + c), (ch, x * 2 + (1 - c))

    def along_y(d):
        return (((y + d + SIDE) % SIDE) * SIDE + z, pr)

    def along_z(d):
        return (y * SIDE + (z + d + SIDE) % SIDE, pr)

    moves = (along_z, along_y)
    live = states_ref[0]

    def at(ref, start, size, cols=None):
        start = pl.multiple_of(start, 16)
        if cols is None:
            return ref.at[pl.ds(start, size)]
        return ref.at[pl.ds(start, size), pl.ds(pl.multiple_of(cols[0], 128), cols[1])]

    count = [0, 0]

    def send(src, dst, device):
        i = count[0]
        count[0] += 1
        copy = pltpu.make_async_remote_copy(
            src_ref=src, dst_ref=dst, send_sem=ssem.at[i], recv_sem=rsem.at[i], device_id=device, device_id_type=MESH
        )
        copy.start()
        started.append(copy)
        return copy

    def local(src, dst):
        i = count[1]
        count[1] += 1
        copy = pltpu.make_async_copy(src, dst, lsem.at[i])
        copy.start()
        return copy

    started = []

    greeted = [near, far, sib, along_y(1), along_y(-1), along_y(2), along_z(1), along_z(-1), along_z(2)]
    barrier = pltpu.get_barrier_semaphore()
    for device in greeted:
        pl.semaphore_signal(barrier, inc=1, device_id=device, device_id_type=MESH)

    mine, theirs_n, theirs_f, theirs_o = pr * rows, (xn * 2 + c) * rows, (xf * 2 + c) * rows, (xo * 2 + c) * rows
    get_eta = local(eta_hbm, eta_left.at[pl.ds(0, rows)])
    tile = width // 4
    get_rec = [local(rec_hbm.at[:, pl.ds(t * tile, tile)], rec.at[:, pl.ds(t * tile, tile)]) for t in range(4)]
    get_om = local(omega_hbm, at(om, mine, rows))
    get_half = local(eta_hbm.at[:, pl.ds(pl.multiple_of(h * half, 128), half)], at(eta_half, mine, rows))

    pl.semaphore_wait(barrier, len(greeted))

    om_near, om_far = [], []
    for r in range(PIECES):
        src = omega_hbm.at[pl.ds(r * sub, sub)]
        dst = at(om, mine + r * sub, sub)
        om_near.append(send(src, dst, near))
        om_far.append(send(src, dst, far))
    om_sib = send(omega_hbm, at(om, mine, rows), sib)
    eh_sib = send(eta_hbm.at[:, pl.ds(pl.multiple_of(h * half, 128), half)], at(eta_half, mine, rows), sib)

    lane = lax.broadcasted_iota(jnp.int32, (8, 128), 1)
    weights = jnp.zeros((8, 128), F32)
    for f in range(map_ref.shape[1]):
        weights += jnp.where(lane == map_ref[0, f], coef_ref[0, f], 0.0)
    wrow[0] = weights
    got_w = []
    for m in range(2):
        for slot, d in ((1, 1), (2, -1), (3, 2)):
            got_w.append(send(wrow.at[0], wrow.at[1 + m * 3 + {1: 2, -1: 1, 2: 3}[d] - 1], moves[m](d)))

    row_no = lax.broadcasted_iota(jnp.int32, (rows, 1), 0)
    col_no = lax.broadcasted_iota(jnp.int32, (1, width), 1)

    def masked(block, first):
        keep = (row_no + first < live) & (col_no < live)
        return jnp.where(keep, block, jnp.zeros((), BF))

    get_eta.wait()
    eta_left[0:rows, :] = masked(eta_left[0:rows, :], mine)
    for t in range(4):
        get_rec[t].wait()
        e_ref[:, t * tile : (t + 1) * tile] = dot(eta_left[0:rows, :], rec[:, t * tile : (t + 1) * tile], NN).astype(BF)
    for t in range(4):
        part = dot(e_ref[...], rec[t * tile : (t + 1) * tile, :], NT)
        keep = lax.broadcasted_iota(jnp.int32, (1, tile), 1) + t * tile < live
        f_ref[:, t * tile : (t + 1) * tile] = jnp.where(keep, part, 0.0).astype(BF)

    om_on, om_near_sib, om_far_sib, om_opp_sib = [], [], [], []

    def pass_on(r):
        om_near[r].wait_recv()
        block = at(om, theirs_n + r * sub, sub)
        om_on.append(send(block, block, far))
        om_near_sib.append(send(block, block, sib))
        om_far[r].wait_recv()
        block = at(om, theirs_f + r * sub, sub)
        om_far_sib.append(send(block, block, sib))

    def pass_opposite(r):
        om_on[r].wait_recv()
        block = at(om, theirs_o + r * sub, sub)
        om_opp_sib.append(send(block, block, sib))

    chips = [x, (x + 1) % SIDE, (x + SIDE - 1) % SIDE, xo]
    quads = {}

    def product(p):
        first = pl.multiple_of(chips[p] * 2 * rows, 16)
        part = dot(f_ref[...], om[pl.ds(first, 2 * rows), :], NT)
        keep = lax.broadcasted_iota(jnp.int32, (1, 2 * rows), 1) + first < live
        part = jnp.where(keep, part, 0.0).astype(BF)
        for m in range(2):
            gath[m, p, 0] = part[:, m * rows : (m + 1) * rows]
            ahead = send(gath.at[m, p, 0], gath.at[m, p, 1], moves[m](turn))
            back = send(gath.at[m, p, 0], gath.at[m, p, 2], moves[m](-turn))
            quads[m, p] = [ahead, back]

    def gather_on(p):
        for m in range(2):
            quads[m, p][0].wait_recv()
            quads[m, p].append(send(gath.at[m, p, 1], gath.at[m, p, 3], moves[m](turn)))

    def weigh(p):
        for m in range(2):
            quads[m, p][1].wait_recv()
            quads[m, p][2].wait_recv()

            def step(i, carry, m=m):
                at_rows = pl.ds(pl.multiple_of(i * sub, 16), sub)
                parts = [gath[m, p, s, at_rows, :].astype(F32) for s in range(4)]
                for t, out in enumerate((own_sum, sum_next, sum_prev, sum_two)):
                    total = sum(wvec[m * 16 + t * 4 + s : m * 16 + t * 4 + s + 1, :] * parts[s] for s in range(4))
                    out[m, p, at_rows, :] = total.astype(out.dtype)
                return carry

            lax.fori_loop(0, PIECES, step, 0)
            other = moves[1 - m]
            two = send(sum_two.at[m, p], merge.at[m, p], other(turn))
            prev = send(sum_prev.at[m, p], fin_a.at[m, p], other(-turn))
            quads[m, p] += [two, prev]

    def merge_on(p):
        for m in range(2):
            quads[m, p][3].wait_recv()
            sum_next[m, p] = (sum_next[m, p].astype(F32) + merge[m, p].astype(F32)).astype(BF)
            quads[m, p].append(send(sum_next.at[m, p], fin_b.at[m, p], moves[1 - m](turn)))

    cross_done = []

    def finish(p):
        for m in range(2):
            quads[m, p][4].wait_recv()
            quads[m, p][5].wait_recv()
            total = own_sum[m, p] + fin_a[m, p].astype(F32) + fin_b[m, p].astype(F32)
            cross_out[m, p] = total.astype(BF)
            first = pl.multiple_of(chips[p] * 2 * rows + m * rows, 128)
            cross_done.append(local(cross_out.at[m, p], cross_hbm.at[:, pl.ds(first, rows)]))

    om_sib.wait_recv()
    get_om.wait()
    product(0)
    pass_on(0)

    for copy in got_w:
        copy.wait_recv()
    for m in range(2):
        for t, d in enumerate((0, turn, -turn, 2)):
            target = along_y(d)[0] if m == 0 else along_z(d)[0]
            for s in range(4):
                if s == 0:
                    row = wrow[0]
                elif s == 3:
                    row = wrow[1 + m * 3 + 2]
                else:
                    plus, minus = wrow[1 + m * 3], wrow[1 + m * 3 + 1]
                    row = jnp.where((turn if s == 2 else -turn) == 1, plus, minus)
                value = jnp.sum(jnp.where(lane == target, row, 0.0), axis=1, keepdims=True)[0:1]
                i = m * 16 + t * 4 + s
                wvec[i : i + 1, :] = jnp.broadcast_to(value, (1, wvec.shape[1]))

    om_left[0:rows, :] = masked(om[pl.ds(pl.multiple_of(mine, 16), rows), :], mine)
    gather_on(0)
    pass_on(1)
    weigh(0)
    pass_on(2)
    merge_on(0)
    pass_on(3)

    eta_n = []

    def eta_to_near(r):
        eta_n.append(send(eta_hbm.at[pl.ds(r * sub, sub)], eta_near.at[pl.ds(r * sub, sub)], near))

    def eta_cols(q, side):
        return pl.ds(pl.multiple_of(side * half + q * quarter, 128), quarter)

    eta_to_near(0)
    for r in range(PIECES):
        om_near_sib[r].wait_recv()
        om_far_sib[r].wait_recv()
    product(1)
    product(2)
    finish(0)
    pass_opposite(0)
    gather_on(1)
    eta_to_near(1)
    pass_opposite(1)
    gather_on(2)
    eta_to_near(2)
    om_left[rows:, :] = masked(om[pl.ds(pl.multiple_of(theirs_n, 16), rows), :], theirs_n)
    weigh(1)
    pass_opposite(2)
    eta_to_near(3)
    weigh(2)
    pass_opposite(3)

    eta_f, eta_on, eta_n_sib, eta_f_sib, eta_o_sib = [], [], [], [], []

    def eta_to_far(q):
        eta_f.append(send(eta_hbm.at[:, eta_cols(q, hf)], at(eta_half, mine, rows, (q * quarter, quarter)), far))

    def eta_pass(q):
        eta_on.append(send(eta_near.at[:, eta_cols(q, hf)], at(eta_half, theirs_n, rows, (q * quarter, quarter)), far))

    eta_to_far(0)
    for r in range(PIECES):
        om_opp_sib[r].wait_recv()
    product(3)
    merge_on(1)
    merge_on(2)
    gather_on(3)

    half_cols = pl.ds(pl.multiple_of(h * half, 128), half)

    def first_term(lo):
        for t in range(half // 512):
            cols = pl.ds(pl.multiple_of(h * half + t * 512, 128), 512)
            acc[lo : lo + rows, t * 512 : (t + 1) * 512] = dot(eta_left[lo : lo + rows, :], om[:, cols], NN)

    first_term(0)
    eta_to_far(1)
    weigh(3)

    for r in range(PIECES):
        eta_n[r].wait_recv()
    eta_pass(0)
    eta_pass(1)
    eta_to_far(2)
    eta_pass(2)
    eta_to_far(3)
    eta_pass(3)
    eta_n_sib = send(eta_near.at[:, half_cols], at(eta_half, theirs_n, rows), sib)
    own_copy = local(eta_near.at[:, half_cols], at(eta_half, theirs_n, rows))
    eta_left[rows:, :] = masked(eta_near[...], theirs_n)
    finish(1)
    finish(2)
    first_term(rows)
    merge_on(3)
    get_half.wait()
    eh_sib.wait_recv()
    eta_n_sib.wait_recv()
    own_copy.wait()

    swaps, pair_done = [], []
    for q in range(PIECES):
        eta_f[q].wait_recv()
        block = at(eta_half, theirs_f, rows, (q * quarter, quarter))
        eta_f_sib.append(send(block, block, sib))
        eta_on[q].wait_recv()
        block = at(eta_half, theirs_o, rows, (q * quarter, quarter))
        eta_o_sib.append(send(block, block, sib))
        if q == 1:
            finish(3)
        eta_f_sib[q].wait_recv()
        eta_o_sib[q].wait_recv()
        cols = slice(q * quarter, (q + 1) * quarter)
        part = acc[:, cols] - dot(om_left[...], eta_half[:, cols], NN)
        keep = lax.broadcasted_iota(jnp.int32, (1, quarter), 1) + h * half + q * quarter < live
        part = jnp.where(keep, part, 0.0).astype(BF)
        pair_send[q] = part[rows:]
        swaps.append(send(pair_send.at[q], pair_out.at[1, q], near))
        pair_out[0, q] = part[:rows]
        pair_done.append(local(pair_out.at[0, q], pair_hbm.at[:, eta_cols(q, h)]))
    for q in range(PIECES):
        swaps[q].wait_recv()
        pair_done.append(local(pair_out.at[1, q], pair_hbm.at[:, eta_cols(q, hf)]))
    for copy in started:
        copy.wait_send()
    for copy in pair_done + cross_done:
        copy.wait()


def body(eta_blocks, omega_blocks, recouple, block_states, cross_map, cross_coef):
    rows, width = eta_blocks.shape[1:]
    half = width // 2
    any_space = pl.BlockSpec(memory_space=pl.ANY)
    smem = pl.BlockSpec(memory_space=pltpu.SMEM)
    square = (2, SIDE, rows, rows)
    out = jax.ShapeDtypeStruct((rows, width), BF)
    pair_comm, cross_comm = pl.pallas_call(
        kernel,
        out_shape=(out, out),
        in_specs=[smem] * 3 + [any_space] * 3,
        out_specs=(any_space, any_space),
        scratch_shapes=[
            pltpu.VMEM((width, width), BF),
            pltpu.VMEM((width, half), BF),
            pltpu.VMEM((2 * rows, width), BF),
            pltpu.VMEM((2 * rows, width), BF),
            pltpu.VMEM((rows, width), BF),
            pltpu.VMEM((width, width), BF),
            pltpu.VMEM((rows, width), BF),
            pltpu.VMEM((rows, width), BF),
            pltpu.VMEM((2, SIDE, SIDE, rows, rows), BF),
            pltpu.VMEM(square, F32),
            pltpu.VMEM(square, BF),
            pltpu.VMEM(square, BF),
            pltpu.VMEM(square, BF),
            pltpu.VMEM(square, BF),
            pltpu.VMEM(square, BF),
            pltpu.VMEM(square, BF),
            pltpu.VMEM((2 * rows, half), F32),
            pltpu.VMEM(square, BF),
            pltpu.VMEM((SIDE, rows, rows), BF),
            pltpu.VMEM(square, BF),
            pltpu.VMEM((7, 8, 128), F32),
            pltpu.VMEM((32, rows), F32),
            pltpu.SemaphoreType.DMA((COPIES,)),
            pltpu.SemaphoreType.DMA((COPIES,)),
            pltpu.SemaphoreType.DMA((32,)),
        ],
        compiler_params=pltpu.CompilerParams(collective_id=0, has_side_effects=True, vmem_limit_bytes=60 * 1024 * 1024),
        cost_estimate=pl.CostEstimate(flops=10 * rows * width * width, bytes_accessed=14 * rows * width * 2, transcendentals=0),
        name="commutators",
    )(block_states, cross_map, cross_coef, eta_blocks[0], omega_blocks[0], recouple[0])
    return pair_comm[None], cross_comm[None]


def solution(mesh):
    placed = (
        P("chan", "pair", None),
        P("chan", "pair", None),
        P("chan", None, None),
        P("chan"),
        P("chan", None),
        P("chan", None),
    )
    return jax.shard_map(
        body,
        mesh=mesh,
        in_specs=placed,
        out_specs=(P("chan", "pair", None), P("chan", "pair", None)),
        check_vma=False,
    )
```

```python
import functools

import jax
import jax.numpy as jnp
from jax import lax
from jax.experimental import pallas as pl
from jax.experimental.pallas import tpu as pltpu
from jax.sharding import PartitionSpec as P

MESH = pl.DeviceIdType.MESH
BF = jnp.bfloat16
F32 = jnp.float32
NN = (((1,), (0,)), ((), ()))
NT = (((1,), (1,)), ((), ()))
SIDE = 4
PIECES = 4
COPIES = 128


def dot(a, b, dims):
    return lax.dot_general(a, b, dims, preferred_element_type=F32)


def kernel(
    states_ref, map_ref, coef_ref, eta_hbm, omega_hbm, rec_hbm, pair_ref, cross_ref,
    om, eta_half, eta_left, om_left, eta_near, rec, e_ref, f_ref,
    gath, own_sum, sum_next, sum_prev, sum_two, merge, fin_a, fin_b,
    acc, pair_send, wrow, wvec,
    ssem, rsem, lsem,
):
    rows, width = eta_hbm.shape
    half = width // 2
    quarter = rows
    sub = rows // PIECES
    ch, pr = lax.axis_index("chan"), lax.axis_index("pair")
    y, z, x, c = ch // SIDE, ch % SIDE, pr // 2, pr % 2
    dn = 1 - 2 * ((x + c) % 2)
    xn, xf, xo = (x + dn + SIDE) % SIDE, (x - dn + SIDE) % SIDE, (x + 2) % SIDE
    turn = 1 - 2 * c
    h = x % 2
    hf = 1 - h
    near, far, sib = (ch, xn * 2 + c), (ch, xf * 2 + c), (ch, x * 2 + (1 - c))

    def along_y(d):
        return (((y + d + SIDE) % SIDE) * SIDE + z, pr)

    def along_z(d):
        return (y * SIDE + (z + d + SIDE) % SIDE, pr)

    moves = (along_z, along_y)
    live = states_ref[0]

    def at(ref, start, size, cols=None):
        start = pl.multiple_of(start, 16)
        if cols is None:
            return ref.at[pl.ds(start, size)]
        return ref.at[pl.ds(start, size), pl.ds(pl.multiple_of(cols[0], 128), cols[1])]

    count = [0, 0]

    def send(src, dst, device):
        i = count[0]
        count[0] += 1
        copy = pltpu.make_async_remote_copy(
            src_ref=src, dst_ref=dst, send_sem=ssem.at[i], recv_sem=rsem.at[i], device_id=device, device_id_type=MESH
        )
        copy.start()
        started.append(copy)
        return copy

    def local(src, dst):
        i = count[1]
        count[1] += 1
        copy = pltpu.make_async_copy(src, dst, lsem.at[i])
        copy.start()
        return copy

    started = []

    greeted = [near, far, sib, along_y(1), along_y(-1), along_y(2), along_z(1), along_z(-1), along_z(2)]
    barrier = pltpu.get_barrier_semaphore()
    for device in greeted:
        pl.semaphore_signal(barrier, inc=1, device_id=device, device_id_type=MESH)

    mine, theirs_n, theirs_f, theirs_o = pr * rows, (xn * 2 + c) * rows, (xf * 2 + c) * rows, (xo * 2 + c) * rows
    get_eta = local(eta_hbm, eta_left.at[pl.ds(0, rows)])
    tile = width // 4
    get_rec = [local(rec_hbm.at[:, pl.ds(t * tile, tile)], rec.at[:, pl.ds(t * tile, tile)]) for t in range(4)]
    get_om = local(omega_hbm, at(om, mine, rows))
    get_half = local(eta_hbm.at[:, pl.ds(pl.multiple_of(h * half, 128), half)], at(eta_half, mine, rows))

    pl.semaphore_wait(barrier, len(greeted))

    om_near, om_far = {}, {}

    def omega_to(r, device, kept):
        kept[r] = send(omega_hbm.at[pl.ds(r * sub, sub)], at(om, mine + r * sub, sub), device)

    for r in range(PIECES):
        omega_to(r, near, om_near)
    om_sib = send(omega_hbm, at(om, mine, rows), sib)
    eh_sib = send(eta_hbm.at[:, pl.ds(pl.multiple_of(h * half, 128), half)], at(eta_half, mine, rows), sib)

    lane = lax.broadcasted_iota(jnp.int32, (8, 128), 1)
    weights = jnp.zeros((8, 128), F32)
    for f in range(map_ref.shape[1]):
        weights += jnp.where(lane == map_ref[0, f], coef_ref[0, f], 0.0)
    wrow[0] = weights
    got_w = []
    for m in range(2):
        for slot, d in ((1, 1), (2, -1), (3, 2)):
            got_w.append(send(wrow.at[0], wrow.at[1 + m * 3 + {1: 2, -1: 1, 2: 3}[d] - 1], moves[m](d)))

    row_no = lax.broadcasted_iota(jnp.int32, (rows, 1), 0)
    col_no = lax.broadcasted_iota(jnp.int32, (1, width), 1)

    def masked(block, first):
        keep = (row_no + first < live) & (col_no < live)
        return jnp.where(keep, block, jnp.zeros((), BF))

    om_on, om_near_sib, om_far_sib, om_opp_sib = {}, {}, {}, {}

    def near_omega(r):
        om_near[r].wait_recv()
        block = at(om, theirs_n + r * sub, sub)
        om_near_sib[r] = send(block, block, sib)

    def omega_to_far(r):
        omega_to(r, far, om_far)

    def far_omega(r):
        om_far[r].wait_recv()
        block = at(om, theirs_f + r * sub, sub)
        om_far_sib[r] = send(block, block, sib)

    def pass_omega(r):
        block = at(om, theirs_n + r * sub, sub)
        om_on[r] = send(block, block, far)

    def opposite_omega(r):
        om_on[r].wait_recv()
        block = at(om, theirs_o + r * sub, sub)
        om_opp_sib[r] = send(block, block, sib)

    def from_sibling(copies):
        for r in range(PIECES):
            copies[r].wait_recv()

    step0 = 1 - 2 * (x % 2)
    chips = [(x, x), ((x + step0 + SIDE) % SIDE, (x - step0 + SIDE) % SIDE), ((x - step0 + SIDE) % SIDE, (x + step0 + SIDE) % SIDE), (xo, xo)]
    quads = {}

    def product(p):
        for m in range(2):
            first = pl.multiple_of((chips[p][m] * 2 + m) * rows, 128)
            part = dot(f_ref[...], om[pl.ds(first, rows), :], NT)
            keep = lax.broadcasted_iota(jnp.int32, (1, rows), 1) + first < live
            gath[m, p, 0] = jnp.where(keep, part, 0.0).astype(BF)
            ahead = send(gath.at[m, p, 0], gath.at[m, p, 1], moves[m](turn))
            back = send(gath.at[m, p, 0], gath.at[m, p, 2], moves[m](-turn))
            quads[m, p] = [ahead, back]

    def gather_on(p):
        for m in range(2):
            quads[m, p][0].wait_recv()
            quads[m, p].append(send(gath.at[m, p, 1], gath.at[m, p, 3], moves[m](turn)))

    def weigh(p):
        for m in range(2):
            quads[m, p][1].wait_recv()
            quads[m, p][2].wait_recv()

            def step(i, carry, m=m):
                at_rows = pl.ds(pl.multiple_of(i * sub, 16), sub)
                parts = [gath[m, p, s, at_rows, :].astype(F32) for s in range(4)]
                for t, out in enumerate((own_sum, sum_next, sum_prev, sum_two)):
                    total = sum(wvec[m * 16 + t * 4 + s : m * 16 + t * 4 + s + 1, :] * parts[s] for s in range(4))
                    out[m, p, at_rows, :] = total.astype(out.dtype)
                return carry

            lax.fori_loop(0, PIECES, step, 0)
            other = moves[1 - m]
            two = send(sum_two.at[m, p], merge.at[m, p], other(turn))
            prev = send(sum_prev.at[m, p], fin_a.at[m, p], other(-turn))
            quads[m, p] += [two, prev]

    def merge_on(p):
        for m in range(2):
            quads[m, p][3].wait_recv()
            sum_next[m, p] = (sum_next[m, p].astype(F32) + merge[m, p].astype(F32)).astype(BF)
            quads[m, p].append(send(sum_next.at[m, p], fin_b.at[m, p], moves[1 - m](turn)))

    def finish(p):
        for m in range(2):
            quads[m, p][4].wait_recv()
            quads[m, p][5].wait_recv()
            total = own_sum[m, p] + fin_a[m, p].astype(F32) + fin_b[m, p].astype(F32)
            first = pl.multiple_of((chips[p][m] * 2 + m) * rows, 128)
            cross_ref[:, pl.ds(first, rows)] = total.astype(BF)

    def recouple():
        get_eta.wait()
        eta_left[0:rows, :] = masked(eta_left[0:rows, :], mine)
        for t in range(4):
            get_rec[t].wait()
            e_ref[:, t * tile : (t + 1) * tile] = dot(eta_left[0:rows, :], rec[:, t * tile : (t + 1) * tile], NN).astype(BF)

    def recouple_back():
        for t in range(4):
            part = dot(e_ref[...], rec[t * tile : (t + 1) * tile, :], NT)
            keep = lax.broadcasted_iota(jnp.int32, (1, tile), 1) + t * tile < live
            f_ref[:, t * tile : (t + 1) * tile] = jnp.where(keep, part, 0.0).astype(BF)

    def own_omega():
        om_sib.wait_recv()
        get_om.wait()

    def set_weights():
        for copy in got_w:
            copy.wait_recv()
        for m in range(2):
            for t, d in enumerate((0, turn, -turn, 2)):
                target = along_y(d)[0] if m == 0 else along_z(d)[0]
                for s in range(4):
                    if s == 0:
                        row = wrow[0]
                    elif s == 3:
                        row = wrow[1 + m * 3 + 2]
                    else:
                        plus, minus = wrow[1 + m * 3], wrow[1 + m * 3 + 1]
                        row = jnp.where((turn if s == 2 else -turn) == 1, plus, minus)
                    value = jnp.sum(jnp.where(lane == target, row, 0.0), axis=1, keepdims=True)[0:1]
                    i = m * 16 + t * 4 + s
                    wvec[i : i + 1, :] = jnp.broadcast_to(value, (1, wvec.shape[1]))

    def own_left():
        om_left[0:rows, :] = masked(om[pl.ds(pl.multiple_of(mine, 16), rows), :], mine)

    def near_left():
        om_left[rows:, :] = masked(om[pl.ds(pl.multiple_of(theirs_n, 16), rows), :], theirs_n)

    eta_n, eta_f, eta_on, eta_f_sib, eta_o_sib, eta_n_sib, own_copy = {}, {}, {}, {}, {}, [], []

    def eta_to_near(r):
        eta_n[r] = send(eta_hbm.at[pl.ds(r * sub, sub)], eta_near.at[pl.ds(r * sub, sub)], near)

    def eta_cols(q, side):
        return pl.ds(pl.multiple_of(side * half + q * quarter, 128), quarter)

    def eta_to_far(q):
        eta_f[q] = send(eta_hbm.at[:, eta_cols(q, hf)], at(eta_half, mine, rows, (q * quarter, quarter)), far)

    def eta_pass(q):
        eta_on[q] = send(eta_near.at[:, eta_cols(q, hf)], at(eta_half, theirs_n, rows, (q * quarter, quarter)), far)

    half_cols = pl.ds(pl.multiple_of(h * half, 128), half)

    def first_term(lo):
        for t in range(half // 512):
            cols = pl.ds(pl.multiple_of(h * half + t * 512, 128), 512)
            acc[lo : lo + rows, t * 512 : (t + 1) * 512] = dot(eta_left[lo : lo + rows, :], om[:, cols], NN)

    def near_eta():
        for r in range(PIECES):
            eta_n[r].wait_recv()

    def share_near_eta():
        eta_n_sib.append(send(eta_near.at[:, half_cols], at(eta_half, theirs_n, rows), sib))
        own_copy.append(local(eta_near.at[:, half_cols], at(eta_half, theirs_n, rows)))
        eta_left[rows:, :] = masked(eta_near[...], theirs_n)

    def settle_eta():
        get_half.wait()
        eh_sib.wait_recv()
        eta_n_sib[0].wait_recv()
        own_copy[0].wait()

    swaps = {}

    def share_eta(q):
        eta_f[q].wait_recv()
        block = at(eta_half, theirs_f, rows, (q * quarter, quarter))
        eta_f_sib[q] = send(block, block, sib)
        eta_on[q].wait_recv()
        block = at(eta_half, theirs_o, rows, (q * quarter, quarter))
        eta_o_sib[q] = send(block, block, sib)

    def last_term(q):
        eta_f_sib[q].wait_recv()
        eta_o_sib[q].wait_recv()
        cols = slice(q * quarter, (q + 1) * quarter)
        part = acc[:, cols] - dot(om_left[...], eta_half[:, cols], NN)
        keep = lax.broadcasted_iota(jnp.int32, (1, quarter), 1) + h * half + q * quarter < live
        part = jnp.where(keep, part, 0.0).astype(BF)
        pair_send[q] = part[rows:]
        swaps[q] = send(pair_send.at[q], pair_ref.at[:, eta_cols(q, h)], near)
        pair_ref[:, eta_cols(q, h)] = part[:rows]

    def swapped(q):
        swaps[q].wait_recv()

    plan = [
        (omega_to_far, 0), (omega_to_far, 3), (recouple,), (own_omega,), (recouple_back,), (omega_to_far, 2), (omega_to_far, 1), (product, 0),
        (near_omega, 1), (near_omega, 0), (pass_omega, 1), (near_omega, 3), (set_weights,), (eta_to_near, 3), (pass_omega, 3), (near_omega, 2),
        (pass_omega, 0), (far_omega, 2), (far_omega, 0), (far_omega, 3), (from_sibling, om_near_sib), (gather_on, 0), (pass_omega, 2), (product, 1),
        (eta_to_near, 0), (far_omega, 1), (eta_to_far, 0), (gather_on, 1), (near_left,), (weigh, 0), (from_sibling, om_far_sib), (product, 2),
        (merge_on, 0), (weigh, 1), (eta_to_near, 2), (opposite_omega, 3), (gather_on, 2), (eta_to_near, 1), (opposite_omega, 1), (opposite_omega, 2),
        (opposite_omega, 0), (from_sibling, om_opp_sib), (product, 3), (eta_to_far, 1), (near_eta,), (eta_pass, 1), (eta_pass, 0), (share_near_eta,),
        (merge_on, 1), (first_term, rows), (gather_on, 3), (eta_to_far, 3), (weigh, 2), (eta_pass, 3), (first_term, 0), (share_eta, 1),
        (eta_to_far, 2), (eta_pass, 2), (own_left,), (settle_eta,), (share_eta, 0), (finish, 0), (weigh, 3), (last_term, 0), (share_eta, 3),
        (last_term, 1), (merge_on, 2), (share_eta, 2), (finish, 1), (last_term, 3), (merge_on, 3), (last_term, 2), (finish, 2), (finish, 3),
        (swapped, 2), (swapped, 1), (swapped, 3), (swapped, 0),
    ]
    for step, *which in plan:
        step(*which)
    for copy in started:
        copy.wait_send()


def body(eta_blocks, omega_blocks, recouple, block_states, cross_map, cross_coef):
    rows, width = eta_blocks.shape[1:]
    half = width // 2
    any_space = pl.BlockSpec(memory_space=pl.ANY)
    smem = pl.BlockSpec(memory_space=pltpu.SMEM)
    square = (2, SIDE, rows, rows)
    out = pltpu.VMEM((rows, width), BF)
    pair_comm, cross_comm = pl.pallas_call(
        kernel,
        out_shape=(out, out),
        in_specs=[smem] * 3 + [any_space] * 3,
        out_specs=(pl.BlockSpec(memory_space=pltpu.VMEM),) * 2,
        scratch_shapes=[
            pltpu.VMEM((width, width), BF),
            pltpu.VMEM((width, half), BF),
            pltpu.VMEM((2 * rows, width), BF),
            pltpu.VMEM((2 * rows, width), BF),
            pltpu.VMEM((rows, width), BF),
            pltpu.VMEM((width, width), BF),
            pltpu.VMEM((rows, width), BF),
            pltpu.VMEM((rows, width), BF),
            pltpu.VMEM((2, SIDE, SIDE, rows, rows), BF),
            pltpu.VMEM(square, F32),
            pltpu.VMEM(square, BF),
            pltpu.VMEM(square, BF),
            pltpu.VMEM(square, BF),
            pltpu.VMEM(square, BF),
            pltpu.VMEM(square, BF),
            pltpu.VMEM(square, BF),
            pltpu.VMEM((2 * rows, half), F32),
            pltpu.VMEM((SIDE, rows, rows), BF),
            pltpu.VMEM((7, 8, 128), F32),
            pltpu.VMEM((32, rows), F32),
            pltpu.SemaphoreType.DMA((COPIES,)),
            pltpu.SemaphoreType.DMA((COPIES,)),
            pltpu.SemaphoreType.DMA((32,)),
        ],
        compiler_params=pltpu.CompilerParams(collective_id=0, has_side_effects=True, vmem_limit_bytes=60 * 1024 * 1024),
        cost_estimate=pl.CostEstimate(flops=10 * rows * width * width, bytes_accessed=14 * rows * width * 2, transcendentals=0),
        name="commutators",
    )(block_states, cross_map, cross_coef, eta_blocks[0], omega_blocks[0], recouple[0])
    return pair_comm[None], cross_comm[None]


def solution(mesh):
    placed = (
        P("chan", "pair", None),
        P("chan", "pair", None),
        P("chan", None, None),
        P("chan"),
        P("chan", None),
        P("chan", None),
    )
    return jax.shard_map(
        body,
        mesh=mesh,
        in_specs=placed,
        out_specs=(P("chan", "pair", None), P("chan", "pair", None)),
        check_vma=False,
    )
```

```python
import functools

import jax
import jax.numpy as jnp
from jax import lax
from jax.experimental import pallas as pl
from jax.experimental.pallas import tpu as pltpu
from jax.sharding import PartitionSpec as P

MESH = pl.DeviceIdType.MESH
BF = jnp.bfloat16
F32 = jnp.float32
NN = (((1,), (0,)), ((), ()))
NT = (((1,), (1,)), ((), ()))
SIDE = 4
PIECES = 4
COPIES = 128


def dot(a, b, dims):
    return lax.dot_general(a, b, dims, preferred_element_type=F32)


def kernel(
    states_ref, map_ref, coef_ref, eta_hbm, omega_hbm, rec_hbm, pair_ref, cross_ref,
    om, eta_half, eta_left, om_left, eta_near, rec, e_ref, f_ref,
    gath, own_sum, sum_next, sum_prev, sum_two, merge, fin_a, fin_b,
    acc, pair_send, wrow, wvec,
    ssem, rsem, lsem, answer, told,
):
    rows, width = eta_hbm.shape
    half = width // 2
    quarter = rows
    sub = rows // PIECES
    ch, pr = lax.axis_index("chan"), lax.axis_index("pair")
    y, z, x, c = ch // SIDE, ch % SIDE, pr // 2, pr % 2
    dn = 1 - 2 * ((x + c) % 2)
    xn, xf, xo = (x + dn + SIDE) % SIDE, (x - dn + SIDE) % SIDE, (x + 2) % SIDE
    turn = 1 - 2 * c
    h = x % 2
    hf = 1 - h
    near, far, sib = (ch, xn * 2 + c), (ch, xf * 2 + c), (ch, x * 2 + (1 - c))

    def along_y(d):
        return (((y + d + SIDE) % SIDE) * SIDE + z, pr)

    def along_z(d):
        return (y * SIDE + (z + d + SIDE) % SIDE, pr)

    moves = (along_z, along_y)
    live = states_ref[0]

    def at(ref, start, size, cols=None):
        start = pl.multiple_of(start, 16)
        if cols is None:
            return ref.at[pl.ds(start, size)]
        return ref.at[pl.ds(start, size), pl.ds(pl.multiple_of(cols[0], 128), cols[1])]

    count = [0, 0]

    def send(src, dst, device):
        i = count[0]
        count[0] += 1
        copy = pltpu.make_async_remote_copy(
            src_ref=src, dst_ref=dst, send_sem=ssem.at[i], recv_sem=rsem.at[i], device_id=device, device_id_type=MESH
        )
        copy.start()
        started.append(copy)
        return copy

    def local(src, dst):
        i = count[1]
        count[1] += 1
        copy = pltpu.make_async_copy(src, dst, lsem.at[i])
        copy.start()
        return copy

    started = []

    barrier = pltpu.get_barrier_semaphore()
    even = (x + c) % 2 == 0
    beside = (near, far, sib)
    across = [move(d) for move in moves for d in (1, -1, 2)]

    def signal(semaphore, device):
        pl.semaphore_signal(semaphore, inc=1, device_id=device, device_id_type=MESH)

    @pl.when(even)
    def _():
        for device in beside:
            signal(barrier, device)

    mine, theirs_n, theirs_f, theirs_o = pr * rows, (xn * 2 + c) * rows, (xf * 2 + c) * rows, (xo * 2 + c) * rows
    get_eta = local(eta_hbm, eta_left.at[pl.ds(0, rows)])
    tile = width // 4
    get_rec = [local(rec_hbm.at[:, pl.ds(t * tile, tile)], rec.at[:, pl.ds(t * tile, tile)]) for t in range(4)]
    get_om = local(omega_hbm, at(om, mine, rows))
    get_half = local(eta_hbm.at[:, pl.ds(pl.multiple_of(h * half, 128), half)], at(eta_half, mine, rows))

    @pl.when(jnp.logical_not(even))
    def _():
        pl.semaphore_wait(barrier, len(beside))
        for device in beside:
            signal(answer, device)

    @pl.when(even)
    def _():
        pl.semaphore_wait(answer, len(beside))

    om_near, om_far = {}, {}

    def omega_to(r, device, kept):
        kept[r] = send(omega_hbm.at[pl.ds(r * sub, sub)], at(om, mine + r * sub, sub), device)

    for r in range(PIECES):
        omega_to(r, near, om_near)
    om_sib = send(omega_hbm, at(om, mine, rows), sib)
    eh_sib = send(eta_hbm.at[:, pl.ds(pl.multiple_of(h * half, 128), half)], at(eta_half, mine, rows), sib)

    lane = lax.broadcasted_iota(jnp.int32, (8, 128), 1)
    weights = jnp.zeros((8, 128), F32)
    for f in range(map_ref.shape[1]):
        weights += jnp.where(lane == map_ref[0, f], coef_ref[0, f], 0.0)
    wrow[0] = weights
    @pl.when(even)
    def _():
        for device in across:
            signal(barrier, device)

    got_w = []

    def meet():
        @pl.when(even)
        def _():
            pl.semaphore_wait(barrier, len(across))
            signal(told, sib)

        @pl.when(jnp.logical_not(even))
        def _():
            pl.semaphore_wait(told, 1)

        for m in range(2):
            for slot, d in ((1, 1), (2, -1), (3, 2)):
                got_w.append(send(wrow.at[0], wrow.at[1 + m * 3 + {1: 2, -1: 1, 2: 3}[d] - 1], moves[m](d)))

    row_no = lax.broadcasted_iota(jnp.int32, (rows, 1), 0)
    col_no = lax.broadcasted_iota(jnp.int32, (1, width), 1)

    def masked(block, first):
        keep = (row_no + first < live) & (col_no < live)
        return jnp.where(keep, block, jnp.zeros((), BF))

    om_on, om_near_sib, om_far_sib, om_opp_sib = {}, {}, {}, {}

    def near_omega(r):
        om_near[r].wait_recv()
        block = at(om, theirs_n + r * sub, sub)
        om_near_sib[r] = send(block, block, sib)

    def omega_to_far(r):
        omega_to(r, far, om_far)

    def far_omega(r):
        om_far[r].wait_recv()
        block = at(om, theirs_f + r * sub, sub)
        om_far_sib[r] = send(block, block, sib)

    def pass_omega(r):
        block = at(om, theirs_n + r * sub, sub)
        om_on[r] = send(block, block, far)

    def opposite_omega(r):
        om_on[r].wait_recv()
        block = at(om, theirs_o + r * sub, sub)
        om_opp_sib[r] = send(block, block, sib)

    def from_sibling(copies):
        for r in range(PIECES):
            copies[r].wait_recv()

    step0 = 1 - 2 * (x % 2)
    chips = [(x, x), ((x + step0 + SIDE) % SIDE, (x - step0 + SIDE) % SIDE), ((x - step0 + SIDE) % SIDE, (x + step0 + SIDE) % SIDE), (xo, xo)]
    quads = {}

    def product(p):
        for m in range(2):
            first = pl.multiple_of((chips[p][m] * 2 + m) * rows, 128)
            part = dot(f_ref[...], om[pl.ds(first, rows), :], NT)
            keep = lax.broadcasted_iota(jnp.int32, (1, rows), 1) + first < live
            gath[m, p, 0] = jnp.where(keep, part, 0.0).astype(BF)
            ahead = send(gath.at[m, p, 0], gath.at[m, p, 1], moves[m](turn))
            back = send(gath.at[m, p, 0], gath.at[m, p, 2], moves[m](-turn))
            quads[m, p] = [ahead, back]

    def gather_on(p):
        for m in range(2):
            quads[m, p][0].wait_recv()
            quads[m, p].append(send(gath.at[m, p, 1], gath.at[m, p, 3], moves[m](turn)))

    def weigh(p):
        for m in range(2):
            quads[m, p][1].wait_recv()
            quads[m, p][2].wait_recv()

            def step(i, carry, m=m):
                at_rows = pl.ds(pl.multiple_of(i * sub, 16), sub)
                parts = [gath[m, p, s, at_rows, :].astype(F32) for s in range(4)]
                for t, out in enumerate((own_sum, sum_next, sum_prev, sum_two)):
                    total = sum(wvec[m * 16 + t * 4 + s : m * 16 + t * 4 + s + 1, :] * parts[s] for s in range(4))
                    out[m, p, at_rows, :] = total.astype(out.dtype)
                return carry

            lax.fori_loop(0, PIECES, step, 0)
            other = moves[1 - m]
            two = send(sum_two.at[m, p], merge.at[m, p], other(turn))
            prev = send(sum_prev.at[m, p], fin_a.at[m, p], other(-turn))
            quads[m, p] += [two, prev]

    def merge_on(p):
        for m in range(2):
            quads[m, p][3].wait_recv()
            sum_next[m, p] = (sum_next[m, p].astype(F32) + merge[m, p].astype(F32)).astype(BF)
            quads[m, p].append(send(sum_next.at[m, p], fin_b.at[m, p], moves[1 - m](turn)))

    def finish(p):
        for m in range(2):
            quads[m, p][4].wait_recv()
            quads[m, p][5].wait_recv()
            total = own_sum[m, p] + fin_a[m, p].astype(F32) + fin_b[m, p].astype(F32)
            first = pl.multiple_of((chips[p][m] * 2 + m) * rows, 128)
            cross_ref[:, pl.ds(first, rows)] = total.astype(BF)

    def recouple():
        get_eta.wait()
        eta_left[0:rows, :] = masked(eta_left[0:rows, :], mine)
        for t in range(4):
            get_rec[t].wait()
            e_ref[:, t * tile : (t + 1) * tile] = dot(eta_left[0:rows, :], rec[:, t * tile : (t + 1) * tile], NN).astype(BF)

    def recouple_back():
        for t in range(4):
            part = dot(e_ref[...], rec[t * tile : (t + 1) * tile, :], NT)
            keep = lax.broadcasted_iota(jnp.int32, (1, tile), 1) + t * tile < live
            f_ref[:, t * tile : (t + 1) * tile] = jnp.where(keep, part, 0.0).astype(BF)

    def own_omega():
        om_sib.wait_recv()
        get_om.wait()

    def set_weights():
        for copy in got_w:
            copy.wait_recv()
        for m in range(2):
            for t, d in enumerate((0, turn, -turn, 2)):
                target = along_y(d)[0] if m == 0 else along_z(d)[0]
                for s in range(4):
                    if s == 0:
                        row = wrow[0]
                    elif s == 3:
                        row = wrow[1 + m * 3 + 2]
                    else:
                        plus, minus = wrow[1 + m * 3], wrow[1 + m * 3 + 1]
                        row = jnp.where((turn if s == 2 else -turn) == 1, plus, minus)
                    value = jnp.sum(jnp.where(lane == target, row, 0.0), axis=1, keepdims=True)[0:1]
                    i = m * 16 + t * 4 + s
                    wvec[i : i + 1, :] = jnp.broadcast_to(value, (1, wvec.shape[1]))

    def own_left():
        om_left[0:rows, :] = masked(om[pl.ds(pl.multiple_of(mine, 16), rows), :], mine)

    def near_left():
        om_left[rows:, :] = masked(om[pl.ds(pl.multiple_of(theirs_n, 16), rows), :], theirs_n)

    eta_n, eta_f, eta_on, eta_f_sib, eta_o_sib, eta_n_sib, own_copy = {}, {}, {}, {}, {}, [], []

    def eta_to_near(r):
        eta_n[r] = send(eta_hbm.at[pl.ds(r * sub, sub)], eta_near.at[pl.ds(r * sub, sub)], near)

    def eta_cols(q, side):
        return pl.ds(pl.multiple_of(side * half + q * quarter, 128), quarter)

    def eta_to_far(q):
        eta_f[q] = send(eta_hbm.at[:, eta_cols(q, hf)], at(eta_half, mine, rows, (q * quarter, quarter)), far)

    def eta_pass(q):
        eta_on[q] = send(eta_near.at[:, eta_cols(q, hf)], at(eta_half, theirs_n, rows, (q * quarter, quarter)), far)

    half_cols = pl.ds(pl.multiple_of(h * half, 128), half)

    def first_term(lo):
        for t in range(half // 512):
            cols = pl.ds(pl.multiple_of(h * half + t * 512, 128), 512)
            acc[lo : lo + rows, t * 512 : (t + 1) * 512] = dot(eta_left[lo : lo + rows, :], om[:, cols], NN)

    def near_eta():
        for r in range(PIECES):
            eta_n[r].wait_recv()

    def share_near_eta():
        eta_n_sib.append(send(eta_near.at[:, half_cols], at(eta_half, theirs_n, rows), sib))
        own_copy.append(local(eta_near.at[:, half_cols], at(eta_half, theirs_n, rows)))
        eta_left[rows:, :] = masked(eta_near[...], theirs_n)

    def settle_eta():
        get_half.wait()
        eh_sib.wait_recv()
        eta_n_sib[0].wait_recv()
        own_copy[0].wait()

    swaps = {}

    def share_eta(q):
        eta_f[q].wait_recv()
        block = at(eta_half, theirs_f, rows, (q * quarter, quarter))
        eta_f_sib[q] = send(block, block, sib)
        eta_on[q].wait_recv()
        block = at(eta_half, theirs_o, rows, (q * quarter, quarter))
        eta_o_sib[q] = send(block, block, sib)

    def last_term(q):
        eta_f_sib[q].wait_recv()
        eta_o_sib[q].wait_recv()
        cols = slice(q * quarter, (q + 1) * quarter)
        part = acc[:, cols] - dot(om_left[...], eta_half[:, cols], NN)
        keep = lax.broadcasted_iota(jnp.int32, (1, quarter), 1) + h * half + q * quarter < live
        part = jnp.where(keep, part, 0.0).astype(BF)
        pair_send[q] = part[rows:]
        swaps[q] = send(pair_send.at[q], pair_ref.at[:, eta_cols(q, h)], near)
        pair_ref[:, eta_cols(q, h)] = part[:rows]

    def swapped(q):
        swaps[q].wait_recv()

    plan = [
        (recouple,), (own_omega,), (recouple_back,), (omega_to_far, 2), (near_omega, 2), (omega_to_far, 1), (omega_to_far, 3), (meet,),
        (near_omega, 1), (near_omega, 0), (product, 0), (near_omega, 3), (omega_to_far, 0), (gather_on, 0), (pass_omega, 1),
        (from_sibling, om_near_sib), (pass_omega, 0), (pass_omega, 3), (product, 1), (set_weights,), (gather_on, 1), (far_omega, 2), (pass_omega, 2),
        (weigh, 0), (far_omega, 1), (far_omega, 3), (far_omega, 0), (weigh, 1), (eta_to_near, 1), (from_sibling, om_far_sib), (product, 2),
        (opposite_omega, 1), (opposite_omega, 0), (own_left,), (merge_on, 0), (opposite_omega, 3), (eta_to_near, 2), (opposite_omega, 2),
        (eta_to_near, 0), (gather_on, 2), (eta_to_near, 3), (merge_on, 1), (from_sibling, om_opp_sib), (product, 3), (near_left,), (finish, 0),
        (first_term, 0), (eta_to_far, 0), (finish, 1), (eta_to_far, 1), (gather_on, 3), (weigh, 2), (near_eta,), (eta_pass, 0), (share_near_eta,),
        (eta_pass, 2), (eta_to_far, 2), (weigh, 3), (eta_pass, 1), (first_term, rows), (share_eta, 0), (eta_to_far, 3), (settle_eta,),
        (share_eta, 2), (eta_pass, 3), (merge_on, 2), (share_eta, 1), (last_term, 0), (merge_on, 3), (last_term, 2), (share_eta, 3), (last_term, 1),
        (swapped, 0), (last_term, 3), (finish, 2), (finish, 3), (swapped, 2), (swapped, 1), (swapped, 3),
    ]
    for step, *which in plan:
        step(*which)
    for copy in started:
        copy.wait_send()


def body(eta_blocks, omega_blocks, recouple, block_states, cross_map, cross_coef):
    rows, width = eta_blocks.shape[1:]
    half = width // 2
    any_space = pl.BlockSpec(memory_space=pl.ANY)
    smem = pl.BlockSpec(memory_space=pltpu.SMEM)
    square = (2, SIDE, rows, rows)
    out = pltpu.VMEM((rows, width), BF)
    pair_comm, cross_comm = pl.pallas_call(
        kernel,
        out_shape=(out, out),
        in_specs=[smem] * 3 + [any_space] * 3,
        out_specs=(pl.BlockSpec(memory_space=pltpu.VMEM),) * 2,
        scratch_shapes=[
            pltpu.VMEM((width, width), BF),
            pltpu.VMEM((width, half), BF),
            pltpu.VMEM((2 * rows, width), BF),
            pltpu.VMEM((2 * rows, width), BF),
            pltpu.VMEM((rows, width), BF),
            pltpu.VMEM((width, width), BF),
            pltpu.VMEM((rows, width), BF),
            pltpu.VMEM((rows, width), BF),
            pltpu.VMEM((2, SIDE, SIDE, rows, rows), BF),
            pltpu.VMEM(square, F32),
            pltpu.VMEM(square, BF),
            pltpu.VMEM(square, BF),
            pltpu.VMEM(square, BF),
            pltpu.VMEM(square, BF),
            pltpu.VMEM(square, BF),
            pltpu.VMEM(square, BF),
            pltpu.VMEM((2 * rows, half), F32),
            pltpu.VMEM((SIDE, rows, rows), BF),
            pltpu.VMEM((7, 8, 128), F32),
            pltpu.VMEM((32, rows), F32),
            pltpu.SemaphoreType.DMA((COPIES,)),
            pltpu.SemaphoreType.DMA((COPIES,)),
            pltpu.SemaphoreType.DMA((32,)),
            pltpu.SemaphoreType.REGULAR,
            pltpu.SemaphoreType.REGULAR,
        ],
        compiler_params=pltpu.CompilerParams(collective_id=0, has_side_effects=True, vmem_limit_bytes=60 * 1024 * 1024),
        cost_estimate=pl.CostEstimate(flops=10 * rows * width * width, bytes_accessed=14 * rows * width * 2, transcendentals=0),
        name="commutators",
    )(block_states, cross_map, cross_coef, eta_blocks[0], omega_blocks[0], recouple[0])
    return pair_comm[None], cross_comm[None]


def solution(mesh):
    placed = (
        P("chan", "pair", None),
        P("chan", "pair", None),
        P("chan", None, None),
        P("chan"),
        P("chan", None),
        P("chan", None),
    )
    return jax.shard_map(
        body,
        mesh=mesh,
        in_specs=placed,
        out_specs=(P("chan", "pair", None), P("chan", "pair", None)),
        check_vma=False,
    )
```

```python
import functools

import jax
import jax.numpy as jnp
from jax import lax
from jax.experimental import pallas as pl
from jax.experimental.pallas import tpu as pltpu
from jax.sharding import PartitionSpec as P

MESH = pl.DeviceIdType.MESH
BF = jnp.bfloat16
F32 = jnp.float32
NN = (((1,), (0,)), ((), ()))
NT = (((1,), (1,)), ((), ()))
SIDE = 4
PIECES = 4
COPIES = 160


def dot(a, b, dims):
    return lax.dot_general(a, b, dims, preferred_element_type=F32)


def kernel(
    states_ref, map_ref, coef_ref, eta_hbm, omega_hbm, rec_hbm, pair_ref, cross_ref,
    om, eta_half, eta_left, om_left, eta_near, rec, e_ref, f_ref,
    gath, own_sum, sum_next, sum_prev, sum_two, merge, fin_a, fin_b,
    acc, pair_send, wrow, wvec,
    ssem, rsem, lsem, answer, told,
):
    rows, width = eta_hbm.shape
    half = width // 2
    quarter = rows
    sub = rows // PIECES
    ch, pr = lax.axis_index("chan"), lax.axis_index("pair")
    y, z, x, c = ch // SIDE, ch % SIDE, pr // 2, pr % 2
    dn = 1 - 2 * ((x + c) % 2)
    xn, xf, xo = (x + dn + SIDE) % SIDE, (x - dn + SIDE) % SIDE, (x + 2) % SIDE
    turn = 1 - 2 * c
    h = x % 2
    hf = 1 - h
    near, far, sib = (ch, xn * 2 + c), (ch, xf * 2 + c), (ch, x * 2 + (1 - c))

    def along_y(d):
        return (((y + d + SIDE) % SIDE) * SIDE + z, pr)

    def along_z(d):
        return (y * SIDE + (z + d + SIDE) % SIDE, pr)

    moves = (along_z, along_y)
    live = states_ref[0]

    def at(ref, start, size, cols=None):
        start = pl.multiple_of(start, 16)
        if cols is None:
            return ref.at[pl.ds(start, size)]
        return ref.at[pl.ds(start, size), pl.ds(pl.multiple_of(cols[0], 128), cols[1])]

    count = [0, 0]

    def send(src, dst, device):
        i = count[0]
        count[0] += 1
        copy = pltpu.make_async_remote_copy(
            src_ref=src, dst_ref=dst, send_sem=ssem.at[i], recv_sem=rsem.at[i], device_id=device, device_id_type=MESH
        )
        copy.start()
        started.append(copy)
        return copy

    def local(src, dst):
        i = count[1]
        count[1] += 1
        copy = pltpu.make_async_copy(src, dst, lsem.at[i])
        copy.start()
        return copy

    started = []

    barrier = pltpu.get_barrier_semaphore()
    even = (x + c) % 2 == 0
    beside = (near, far, sib)
    across = [move(d) for move in moves for d in (1, -1, 2)]

    def signal(semaphore, device):
        pl.semaphore_signal(semaphore, inc=1, device_id=device, device_id_type=MESH)

    @pl.when(even)
    def _():
        for device in beside:
            signal(barrier, device)

    mine, theirs_n, theirs_f, theirs_o = pr * rows, (xn * 2 + c) * rows, (xf * 2 + c) * rows, (xo * 2 + c) * rows
    get_eta = local(eta_hbm, eta_left.at[pl.ds(0, rows)])
    tile = width // 4
    get_rec = [local(rec_hbm.at[:, pl.ds(t * tile, tile)], rec.at[:, pl.ds(t * tile, tile)]) for t in range(4)]
    get_om = local(omega_hbm, at(om, mine, rows))
    get_half = local(eta_hbm.at[:, pl.ds(pl.multiple_of(h * half, 128), half)], at(eta_half, mine, rows))

    @pl.when(jnp.logical_not(even))
    def _():
        pl.semaphore_wait(barrier, len(beside))
        for device in beside:
            signal(answer, device)

    @pl.when(even)
    def _():
        pl.semaphore_wait(answer, len(beside))

    om_near, om_far = {}, {}

    def omega_to(r, device, kept):
        kept[r] = send(omega_hbm.at[pl.ds(r * sub, sub)], at(om, mine + r * sub, sub), device)

    for r in range(PIECES):
        omega_to(r, near, om_near)
    om_sib = send(omega_hbm, at(om, mine, rows), sib)
    eh_sib = send(eta_hbm.at[:, pl.ds(pl.multiple_of(h * half, 128), half)], at(eta_half, mine, rows), sib)

    lane = lax.broadcasted_iota(jnp.int32, (8, 128), 1)
    weights = jnp.zeros((8, 128), F32)
    for f in range(map_ref.shape[1]):
        weights += jnp.where(lane == map_ref[0, f], coef_ref[0, f], 0.0)
    wrow[0] = weights
    @pl.when(even)
    def _():
        for device in across:
            signal(barrier, device)

    got_w = []

    def meet():
        @pl.when(even)
        def _():
            pl.semaphore_wait(barrier, len(across))
            signal(told, sib)

        @pl.when(jnp.logical_not(even))
        def _():
            pl.semaphore_wait(told, 1)

        for m in range(2):
            for slot, d in ((1, 1), (2, -1), (3, 2)):
                got_w.append(send(wrow.at[0], wrow.at[1 + m * 3 + {1: 2, -1: 1, 2: 3}[d] - 1], moves[m](d)))

    row_no = lax.broadcasted_iota(jnp.int32, (rows, 1), 0)
    col_no = lax.broadcasted_iota(jnp.int32, (1, width), 1)

    def masked(block, first):
        keep = (row_no + first < live) & (col_no < live)
        return jnp.where(keep, block, jnp.zeros((), BF))

    om_on, om_near_sib, om_far_sib, om_opp_sib = {}, {}, {}, {}

    def near_omega(r):
        om_near[r].wait_recv()
        block = at(om, theirs_n + r * sub, sub)
        om_near_sib[r] = send(block, block, sib)

    def omega_to_far(r):
        omega_to(r, far, om_far)

    def far_omega(r):
        om_far[r].wait_recv()
        block = at(om, theirs_f + r * sub, sub)
        om_far_sib[r] = send(block, block, sib)

    def pass_omega(r):
        block = at(om, theirs_n + r * sub, sub)
        om_on[r] = send(block, block, far)

    def opposite_omega(r):
        om_on[r].wait_recv()
        block = at(om, theirs_o + r * sub, sub)
        om_opp_sib[r] = send(block, block, sib)

    def from_sibling(copies):
        for r in range(PIECES):
            copies[r].wait_recv()

    step0 = 1 - 2 * (x % 2)
    chips = [(x, x), ((x + step0 + SIDE) % SIDE, (x - step0 + SIDE) % SIDE), ((x - step0 + SIDE) % SIDE, (x + step0 + SIDE) % SIDE), (xo, xo)]
    parts_of = [(0, 0, rows), (1, 0, rows), (2, 0, rows), (3, 0, rows // 2), (3, rows // 2, rows // 2)]
    quads = {}

    def start_of(p, m):
        k, lo, _ = parts_of[p]
        return pl.multiple_of((chips[k][m] * 2 + m) * rows + lo, 128)

    def cut(ref, p, *index):
        k, lo, size = parts_of[p]
        return ref.at[index[0], k, *index[1:], :, pl.ds(lo, size)]

    def product(p):
        size = parts_of[p][2]
        if p >= 3:
            for r in range((p - 3) * 2, (p - 3) * 2 + 2):
                om_opp_sib[r].wait_recv()
        for m in range(2):
            first = start_of(p, m)
            part = dot(f_ref[...], om[pl.ds(first, size), :], NT)
            keep = lax.broadcasted_iota(jnp.int32, (1, size), 1) + first < live
            cut(gath, p, m, 0)[...] = jnp.where(keep, part, 0.0).astype(BF)
            ahead = send(cut(gath, p, m, 0), cut(gath, p, m, 1), moves[m](turn))
            back = send(cut(gath, p, m, 0), cut(gath, p, m, 2), moves[m](-turn))
            quads[m, p] = [ahead, back]

    def gather_on(p):
        for m in range(2):
            quads[m, p][0].wait_recv()
            quads[m, p].append(send(cut(gath, p, m, 1), cut(gath, p, m, 3), moves[m](turn)))

    def weigh(p):
        for m in range(2):
            quads[m, p][1].wait_recv()
            quads[m, p][2].wait_recv()

            k, lo, size = parts_of[p]
            cols = pl.ds(lo, size)

            def step(i, carry, m=m, k=k, cols=cols, size=size):
                at_rows = pl.ds(pl.multiple_of(i * sub, 16), sub)
                parts = [gath[m, k, s, at_rows, cols].astype(F32) for s in range(4)]
                for t, out in enumerate((own_sum, sum_next, sum_prev, sum_two)):
                    total = sum(wvec[m * 16 + t * 4 + s : m * 16 + t * 4 + s + 1, 0:size] * parts[s] for s in range(4))
                    out[m, k, at_rows, cols] = total.astype(out.dtype)
                return carry

            lax.fori_loop(0, PIECES, step, 0)
            other = moves[1 - m]
            two = send(cut(sum_two, p, m), cut(merge, p, m), other(turn))
            prev = send(cut(sum_prev, p, m), cut(fin_a, p, m), other(-turn))
            quads[m, p] += [two, prev]

    def merge_on(p):
        for m in range(2):
            quads[m, p][3].wait_recv()
            ahead = cut(sum_next, p, m)
            ahead[...] = (ahead[...].astype(F32) + cut(merge, p, m)[...].astype(F32)).astype(BF)
            quads[m, p].append(send(ahead, cut(fin_b, p, m), moves[1 - m](turn)))

    def finish(p):
        for m in range(2):
            quads[m, p][4].wait_recv()
            quads[m, p][5].wait_recv()
            total = cut(own_sum, p, m)[...] + cut(fin_a, p, m)[...].astype(F32) + cut(fin_b, p, m)[...].astype(F32)
            cross_ref[:, pl.ds(start_of(p, m), parts_of[p][2])] = total.astype(BF)

    def recouple():
        get_eta.wait()
        eta_left[0:rows, :] = masked(eta_left[0:rows, :], mine)
        for t in range(4):
            get_rec[t].wait()
            e_ref[:, t * tile : (t + 1) * tile] = dot(eta_left[0:rows, :], rec[:, t * tile : (t + 1) * tile], NN).astype(BF)

    def recouple_back():
        for t in range(4):
            part = dot(e_ref[...], rec[t * tile : (t + 1) * tile, :], NT)
            keep = lax.broadcasted_iota(jnp.int32, (1, tile), 1) + t * tile < live
            f_ref[:, t * tile : (t + 1) * tile] = jnp.where(keep, part, 0.0).astype(BF)

    def own_omega():
        om_sib.wait_recv()
        get_om.wait()

    def set_weights():
        for copy in got_w:
            copy.wait_recv()
        for m in range(2):
            for t, d in enumerate((0, turn, -turn, 2)):
                target = along_y(d)[0] if m == 0 else along_z(d)[0]
                for s in range(4):
                    if s == 0:
                        row = wrow[0]
                    elif s == 3:
                        row = wrow[1 + m * 3 + 2]
                    else:
                        plus, minus = wrow[1 + m * 3], wrow[1 + m * 3 + 1]
                        row = jnp.where((turn if s == 2 else -turn) == 1, plus, minus)
                    value = jnp.sum(jnp.where(lane == target, row, 0.0), axis=1, keepdims=True)[0:1]
                    i = m * 16 + t * 4 + s
                    wvec[i : i + 1, :] = jnp.broadcast_to(value, (1, wvec.shape[1]))

    def own_left():
        om_left[0:rows, :] = masked(om[pl.ds(pl.multiple_of(mine, 16), rows), :], mine)

    def near_left():
        om_left[rows:, :] = masked(om[pl.ds(pl.multiple_of(theirs_n, 16), rows), :], theirs_n)

    eta_n, eta_f, eta_on, eta_f_sib, eta_o_sib, eta_n_sib, own_copy = {}, {}, {}, {}, {}, [], []

    def eta_to_near(r):
        side, first = (h, r) if r < 2 else (hf, r - 2)
        cols = pl.ds(pl.multiple_of(side * half + first * 2 * quarter, 128), 2 * quarter)
        eta_n[r] = send(eta_hbm.at[:, cols], eta_near.at[:, cols], near)

    def eta_cols(q, side):
        return pl.ds(pl.multiple_of(side * half + q * quarter, 128), quarter)

    def eta_to_far(q):
        eta_f[q] = send(eta_hbm.at[:, eta_cols(q, hf)], at(eta_half, mine, rows, (q * quarter, quarter)), far)

    def eta_pass(q):
        eta_on[q] = send(eta_near.at[:, eta_cols(q, hf)], at(eta_half, theirs_n, rows, (q * quarter, quarter)), far)

    half_cols = pl.ds(pl.multiple_of(h * half, 128), half)

    def first_term(lo):
        for t in range(half // 512):
            cols = pl.ds(pl.multiple_of(h * half + t * 512, 128), 512)
            acc[lo : lo + rows, t * 512 : (t + 1) * 512] = dot(eta_left[lo : lo + rows, :], om[:, cols], NN)

    def near_eta(r):
        eta_n[r].wait_recv()

    def share_near_eta():
        eta_n_sib.append(send(eta_near.at[:, half_cols], at(eta_half, theirs_n, rows), sib))
        own_copy.append(local(eta_near.at[:, half_cols], at(eta_half, theirs_n, rows)))
        eta_left[rows:, :] = masked(eta_near[...], theirs_n)

    def settle_eta():
        get_half.wait()
        eh_sib.wait_recv()
        eta_n_sib[0].wait_recv()
        own_copy[0].wait()

    swaps = {}

    def share_eta(q):
        eta_f[q].wait_recv()
        block = at(eta_half, theirs_f, rows, (q * quarter, quarter))
        eta_f_sib[q] = send(block, block, sib)
        eta_on[q].wait_recv()
        block = at(eta_half, theirs_o, rows, (q * quarter, quarter))
        eta_o_sib[q] = send(block, block, sib)

    def last_term(q):
        eta_f_sib[q].wait_recv()
        eta_o_sib[q].wait_recv()
        cols = slice(q * quarter, (q + 1) * quarter)
        part = acc[:, cols] - dot(om_left[...], eta_half[:, cols], NN)
        keep = lax.broadcasted_iota(jnp.int32, (1, quarter), 1) + h * half + q * quarter < live
        part = jnp.where(keep, part, 0.0).astype(BF)
        pair_send[q] = part[rows:]
        swaps[q] = send(pair_send.at[q], pair_ref.at[:, eta_cols(q, h)], near)
        pair_ref[:, eta_cols(q, h)] = part[:rows]

    def swapped(q):
        swaps[q].wait_recv()

    plan = [
        (recouple,), (meet,), (own_omega,), (own_left,), (omega_to_far, 1), (recouple_back,), (omega_to_far, 0), (product, 0), (omega_to_far, 3),
        (omega_to_far, 2), (near_omega, 2), (near_omega, 3), (pass_omega, 3), (near_omega, 0), (near_omega, 1), (gather_on, 0), (pass_omega, 1),
        (from_sibling, om_near_sib), (set_weights,), (pass_omega, 0), (product, 1), (weigh, 0), (far_omega, 0), (far_omega, 2), (gather_on, 1),
        (far_omega, 3), (pass_omega, 2), (merge_on, 0), (far_omega, 1), (eta_to_near, 0), (weigh, 1), (eta_to_near, 3), (opposite_omega, 0),
        (eta_to_far, 1), (from_sibling, om_far_sib), (opposite_omega, 3), (opposite_omega, 1), (product, 2), (product, 3), (eta_to_near, 2),
        (eta_to_near, 1), (near_left,), (merge_on, 1), (opposite_omega, 2), (near_eta, 0), (gather_on, 2), (product, 4), (gather_on, 3),
        (first_term, 0), (eta_pass, 0), (eta_pass, 1), (eta_to_far, 0), (gather_on, 4), (weigh, 3), (near_eta, 1), (near_eta, 3), (near_eta, 2),
        (eta_pass, 3), (weigh, 2), (share_near_eta,), (eta_to_far, 3), (weigh, 4), (share_eta, 0), (eta_pass, 2), (finish, 0), (eta_to_far, 2),
        (share_eta, 1), (first_term, rows), (settle_eta,), (last_term, 0), (share_eta, 3), (merge_on, 3), (last_term, 1), (share_eta, 2),
        (merge_on, 4), (merge_on, 2), (last_term, 3), (last_term, 2), (finish, 3), (finish, 1), (finish, 4), (swapped, 1), (swapped, 3), (finish, 2),
        (swapped, 0), (swapped, 2),
    ]
    for step, *which in plan:
        step(*which)
    for copy in started:
        copy.wait_send()


def body(eta_blocks, omega_blocks, recouple, block_states, cross_map, cross_coef):
    rows, width = eta_blocks.shape[1:]
    half = width // 2
    any_space = pl.BlockSpec(memory_space=pl.ANY)
    smem = pl.BlockSpec(memory_space=pltpu.SMEM)
    square = (2, SIDE, rows, rows)
    out = pltpu.VMEM((rows, width), BF)
    pair_comm, cross_comm = pl.pallas_call(
        kernel,
        out_shape=(out, out),
        in_specs=[smem] * 3 + [any_space] * 3,
        out_specs=(pl.BlockSpec(memory_space=pltpu.VMEM),) * 2,
        scratch_shapes=[
            pltpu.VMEM((width, width), BF),
            pltpu.VMEM((width, half), BF),
            pltpu.VMEM((2 * rows, width), BF),
            pltpu.VMEM((2 * rows, width), BF),
            pltpu.VMEM((rows, width), BF),
            pltpu.VMEM((width, width), BF),
            pltpu.VMEM((rows, width), BF),
            pltpu.VMEM((rows, width), BF),
            pltpu.VMEM((2, SIDE, SIDE, rows, rows), BF),
            pltpu.VMEM(square, F32),
            pltpu.VMEM(square, BF),
            pltpu.VMEM(square, BF),
            pltpu.VMEM(square, BF),
            pltpu.VMEM(square, BF),
            pltpu.VMEM(square, BF),
            pltpu.VMEM(square, BF),
            pltpu.VMEM((2 * rows, half), F32),
            pltpu.VMEM((SIDE, rows, rows), BF),
            pltpu.VMEM((7, 8, 128), F32),
            pltpu.VMEM((32, rows), F32),
            pltpu.SemaphoreType.DMA((COPIES,)),
            pltpu.SemaphoreType.DMA((COPIES,)),
            pltpu.SemaphoreType.DMA((32,)),
            pltpu.SemaphoreType.REGULAR,
            pltpu.SemaphoreType.REGULAR,
        ],
        compiler_params=pltpu.CompilerParams(collective_id=0, has_side_effects=True, vmem_limit_bytes=60 * 1024 * 1024),
        cost_estimate=pl.CostEstimate(flops=10 * rows * width * width, bytes_accessed=14 * rows * width * 2, transcendentals=0),
        name="commutators",
    )(block_states, cross_map, cross_coef, eta_blocks[0], omega_blocks[0], recouple[0])
    return pair_comm[None], cross_comm[None]


def solution(mesh):
    placed = (
        P("chan", "pair", None),
        P("chan", "pair", None),
        P("chan", None, None),
        P("chan"),
        P("chan", None),
        P("chan", None),
    )
    return jax.shard_map(
        body,
        mesh=mesh,
        in_specs=placed,
        out_specs=(P("chan", "pair", None), P("chan", "pair", None)),
        check_vma=False,
    )
```

```python
import functools

import jax
import jax.numpy as jnp
from jax import lax
from jax.experimental import pallas as pl
from jax.experimental.pallas import tpu as pltpu
from jax.sharding import PartitionSpec as P

MESH = pl.DeviceIdType.MESH
BF = jnp.bfloat16
F32 = jnp.float32
NN = (((1,), (0,)), ((), ()))
NT = (((1,), (1,)), ((), ()))
SIDE = 4
PIECES = 4
COPIES = 160


def dot(a, b, dims):
    return lax.dot_general(a, b, dims, preferred_element_type=F32)


def kernel(
    states_ref, map_ref, coef_ref, eta_hbm, omega_hbm, rec_hbm, pair_ref, cross_ref,
    om, eta_half, eta_left, om_left, eta_near, rec, e_ref, f_ref,
    gath, own_sum, sum_next, sum_prev, sum_two, merge, fin_a, fin_b,
    acc, pair_send, wrow, wvec,
    ssem, rsem, lsem, answer, told,
):
    rows, width = eta_hbm.shape
    half = width // 2
    quarter = rows
    sub = rows // PIECES
    ch, pr = lax.axis_index("chan"), lax.axis_index("pair")
    y, z, x, c = ch // SIDE, ch % SIDE, pr // 2, pr % 2
    dn = 1 - 2 * ((x + c) % 2)
    xn, xf, xo = (x + dn + SIDE) % SIDE, (x - dn + SIDE) % SIDE, (x + 2) % SIDE
    turn = 1 - 2 * c
    h = x % 2
    hf = 1 - h
    near, far, sib = (ch, xn * 2 + c), (ch, xf * 2 + c), (ch, x * 2 + (1 - c))

    def along_y(d):
        return (((y + d + SIDE) % SIDE) * SIDE + z, pr)

    def along_z(d):
        return (y * SIDE + (z + d + SIDE) % SIDE, pr)

    moves = (along_z, along_y)
    live = states_ref[0]

    def at(ref, start, size, cols=None):
        start = pl.multiple_of(start, 16)
        if cols is None:
            return ref.at[pl.ds(start, size)]
        return ref.at[pl.ds(start, size), pl.ds(pl.multiple_of(cols[0], 128), cols[1])]

    count = [0, 0]

    def send(src, dst, device):
        i = count[0]
        count[0] += 1
        copy = pltpu.make_async_remote_copy(
            src_ref=src, dst_ref=dst, send_sem=ssem.at[i], recv_sem=rsem.at[i], device_id=device, device_id_type=MESH
        )
        copy.start()
        started.append(copy)
        return copy

    def local(src, dst):
        i = count[1]
        count[1] += 1
        copy = pltpu.make_async_copy(src, dst, lsem.at[i])
        copy.start()
        return copy

    started = []

    barrier = pltpu.get_barrier_semaphore()
    even = (x + c) % 2 == 0
    beside = (near, far, sib)
    across = [move(d) for move in moves for d in (1, -1, 2)]

    def signal(semaphore, device):
        pl.semaphore_signal(semaphore, inc=1, device_id=device, device_id_type=MESH)

    @pl.when(even)
    def _():
        for device in beside:
            signal(barrier, device)

    mine, theirs_n, theirs_f, theirs_o = pr * rows, (xn * 2 + c) * rows, (xf * 2 + c) * rows, (xo * 2 + c) * rows
    get_eta = local(eta_hbm, eta_left.at[pl.ds(0, rows)])
    tile = width // 4
    get_rec = [local(rec_hbm.at[:, pl.ds(t * tile, tile)], rec.at[:, pl.ds(t * tile, tile)]) for t in range(4)]
    get_om = local(omega_hbm, at(om, mine, rows))
    get_half = local(eta_hbm.at[:, pl.ds(pl.multiple_of(h * half, 128), half)], at(eta_half, mine, rows))

    @pl.when(jnp.logical_not(even))
    def _():
        pl.semaphore_wait(barrier, len(beside))
        for device in beside:
            signal(answer, device)

    @pl.when(even)
    def _():
        pl.semaphore_wait(answer, len(beside))

    om_near, om_far = {}, {}

    def omega_to(r, device, kept):
        kept[r] = send(omega_hbm.at[pl.ds(r * sub, sub)], at(om, mine + r * sub, sub), device)

    for r in range(PIECES):
        omega_to(r, near, om_near)
    om_sib = send(omega_hbm, at(om, mine, rows), sib)
    eh_sib = send(eta_hbm.at[:, pl.ds(pl.multiple_of(h * half, 128), half)], at(eta_half, mine, rows), sib)

    lane = lax.broadcasted_iota(jnp.int32, (8, 128), 1)
    weights = jnp.zeros((8, 128), F32)
    for f in range(map_ref.shape[1]):
        weights += jnp.where(lane == map_ref[0, f], coef_ref[0, f], 0.0)
    wrow[0] = weights
    @pl.when(even)
    def _():
        for device in across:
            signal(barrier, device)

    got_w = []

    def meet():
        @pl.when(even)
        def _():
            pl.semaphore_wait(barrier, len(across))
            signal(told, sib)

        @pl.when(jnp.logical_not(even))
        def _():
            pl.semaphore_wait(told, 1)

        for m in range(2):
            for slot, d in ((1, 1), (2, -1), (3, 2)):
                got_w.append(send(wrow.at[0], wrow.at[1 + m * 3 + {1: 2, -1: 1, 2: 3}[d] - 1], moves[m](d)))

    row_no = lax.broadcasted_iota(jnp.int32, (rows, 1), 0)
    col_no = lax.broadcasted_iota(jnp.int32, (1, width), 1)

    def masked(block, first):
        keep = (row_no + first < live) & (col_no < live)
        return jnp.where(keep, block, jnp.zeros((), BF))

    om_on, om_near_sib, om_far_sib, om_opp_sib = {}, {}, {}, {}

    def near_omega(r):
        om_near[r].wait_recv()
        block = at(om, theirs_n + r * sub, sub)
        om_near_sib[r] = send(block, block, sib)

    def omega_to_far(r):
        omega_to(r, far, om_far)

    def far_omega(r):
        om_far[r].wait_recv()
        block = at(om, theirs_f + r * sub, sub)
        om_far_sib[r] = send(block, block, sib)

    def pass_omega(r):
        block = at(om, theirs_n + r * sub, sub)
        om_on[r] = send(block, block, far)

    def opposite_omega(r):
        om_on[r].wait_recv()
        block = at(om, theirs_o + r * sub, sub)
        om_opp_sib[r] = send(block, block, sib)

    def from_sibling(copies):
        for r in range(PIECES):
            copies[r].wait_recv()

    step0 = 1 - 2 * (x % 2)
    chips = [(x, x), ((x + step0 + SIDE) % SIDE, (x - step0 + SIDE) % SIDE), ((x - step0 + SIDE) % SIDE, (x + step0 + SIDE) % SIDE), (xo, xo)]
    parts_of = [(0, 0, rows), (1, 0, rows), (2, 0, rows), (3, 0, rows // 2), (3, rows // 2, rows // 2)]
    quads = {}

    def start_of(p, m):
        k, lo, _ = parts_of[p]
        return pl.multiple_of((chips[k][m] * 2 + m) * rows + lo, 128)

    def cut(ref, p, *index):
        k, lo, size = parts_of[p]
        return ref.at[index[0], k, *index[1:], :, pl.ds(lo, size)]

    def product(p):
        size = parts_of[p][2]
        if p >= 3:
            for r in range((p - 3) * 2, (p - 3) * 2 + 2):
                om_opp_sib[r].wait_recv()
        for m in range(2):
            first = start_of(p, m)
            part = dot(f_ref[...], om[pl.ds(first, size), :], NT)
            keep = lax.broadcasted_iota(jnp.int32, (1, size), 1) + first < live
            cut(gath, p, m, 0)[...] = jnp.where(keep, part, 0.0).astype(BF)
            ahead = send(cut(gath, p, m, 0), cut(gath, p, m, 1), moves[m](turn))
            back = send(cut(gath, p, m, 0), cut(gath, p, m, 2), moves[m](-turn))
            quads[m, p] = [ahead, back]

    def gather_on(p):
        for m in range(2):
            quads[m, p][0].wait_recv()
            quads[m, p].append(send(cut(gath, p, m, 1), cut(gath, p, m, 3), moves[m](turn)))

    def weigh(p):
        for m in range(2):
            quads[m, p][1].wait_recv()
            quads[m, p][2].wait_recv()

            k, lo, size = parts_of[p]
            cols = pl.ds(lo, size)

            def step(i, carry, m=m, k=k, cols=cols, size=size):
                at_rows = pl.ds(pl.multiple_of(i * sub, 16), sub)
                parts = [gath[m, k, s, at_rows, cols].astype(F32) for s in range(4)]
                for t, out in enumerate((own_sum, sum_next, sum_prev, sum_two)):
                    total = sum(wvec[m * 16 + t * 4 + s : m * 16 + t * 4 + s + 1, 0:size] * parts[s] for s in range(4))
                    out[m, k, at_rows, cols] = total.astype(out.dtype)
                return carry

            lax.fori_loop(0, PIECES, step, 0)
            other = moves[1 - m]
            two = send(cut(sum_two, p, m), cut(merge, p, m), other(turn))
            prev = send(cut(sum_prev, p, m), cut(fin_a, p, m), other(-turn))
            quads[m, p] += [two, prev]

    def merge_on(p):
        for m in range(2):
            quads[m, p][3].wait_recv()
            ahead = cut(sum_next, p, m)
            ahead[...] = (ahead[...].astype(F32) + cut(merge, p, m)[...].astype(F32)).astype(BF)
            quads[m, p].append(send(ahead, cut(fin_b, p, m), moves[1 - m](turn)))

    def finish(p):
        for m in range(2):
            quads[m, p][4].wait_recv()
            quads[m, p][5].wait_recv()
            total = cut(own_sum, p, m)[...] + cut(fin_a, p, m)[...].astype(F32) + cut(fin_b, p, m)[...].astype(F32)
            cross_ref[:, pl.ds(start_of(p, m), parts_of[p][2])] = total.astype(BF)

    def recouple():
        get_eta.wait()
        eta_left[0:rows, :] = masked(eta_left[0:rows, :], mine)
        for t in range(4):
            get_rec[t].wait()
            e_ref[:, t * tile : (t + 1) * tile] = dot(eta_left[0:rows, :], rec[:, t * tile : (t + 1) * tile], NN).astype(BF)

    def recouple_back():
        for t in range(4):
            part = dot(e_ref[...], rec[t * tile : (t + 1) * tile, :], NT)
            keep = lax.broadcasted_iota(jnp.int32, (1, tile), 1) + t * tile < live
            f_ref[:, t * tile : (t + 1) * tile] = jnp.where(keep, part, 0.0).astype(BF)

    def own_omega():
        om_sib.wait_recv()
        get_om.wait()

    def set_weights():
        for copy in got_w:
            copy.wait_recv()
        for m in range(2):
            for t, d in enumerate((0, turn, -turn, 2)):
                target = along_y(d)[0] if m == 0 else along_z(d)[0]
                for s in range(4):
                    if s == 0:
                        row = wrow[0]
                    elif s == 3:
                        row = wrow[1 + m * 3 + 2]
                    else:
                        plus, minus = wrow[1 + m * 3], wrow[1 + m * 3 + 1]
                        row = jnp.where((turn if s == 2 else -turn) == 1, plus, minus)
                    value = jnp.sum(jnp.where(lane == target, row, 0.0), axis=1, keepdims=True)[0:1]
                    i = m * 16 + t * 4 + s
                    wvec[i : i + 1, :] = jnp.broadcast_to(value, (1, wvec.shape[1]))

    def own_left():
        om_left[0:rows, :] = masked(om[pl.ds(pl.multiple_of(mine, 16), rows), :], mine)

    def near_left():
        om_left[rows:, :] = masked(om[pl.ds(pl.multiple_of(theirs_n, 16), rows), :], theirs_n)

    eta_n, eta_f, eta_on, eta_f_sib, eta_o_sib, eta_n_sib, own_copy = {}, {}, {}, {}, {}, [], []

    def eta_to_near(r):
        side, first = (h, r) if r < 2 else (hf, r - 2)
        cols = pl.ds(pl.multiple_of(side * half + first * 2 * quarter, 128), 2 * quarter)
        eta_n[r] = send(eta_hbm.at[:, cols], eta_near.at[:, cols], near)

    def eta_cols(q, side):
        return pl.ds(pl.multiple_of(side * half + q * quarter, 128), quarter)

    def eta_to_far(q):
        eta_f[q] = send(eta_hbm.at[:, eta_cols(q, hf)], at(eta_half, mine, rows, (q * quarter, quarter)), far)

    def eta_pass(q):
        eta_on[q] = send(eta_near.at[:, eta_cols(q, hf)], at(eta_half, theirs_n, rows, (q * quarter, quarter)), far)

    half_cols = pl.ds(pl.multiple_of(h * half, 128), half)

    def first_term(lo):
        for t in range(half // 512):
            cols = pl.ds(pl.multiple_of(h * half + t * 512, 128), 512)
            acc[lo : lo + rows, t * 512 : (t + 1) * 512] = dot(eta_left[lo : lo + rows, :], om[:, cols], NN)

    def near_eta(r):
        eta_n[r].wait_recv()

    def share_near_eta():
        eta_n_sib.append(send(eta_near.at[:, half_cols], at(eta_half, theirs_n, rows), sib))
        own_copy.append(local(eta_near.at[:, half_cols], at(eta_half, theirs_n, rows)))
        eta_left[rows:, :] = masked(eta_near[...], theirs_n)

    def settle_eta():
        get_half.wait()
        eh_sib.wait_recv()
        eta_n_sib[0].wait_recv()
        own_copy[0].wait()

    swaps = {}

    def share_eta(q):
        eta_f[q].wait_recv()
        block = at(eta_half, theirs_f, rows, (q * quarter, quarter))
        eta_f_sib[q] = send(block, block, sib)
        eta_on[q].wait_recv()
        block = at(eta_half, theirs_o, rows, (q * quarter, quarter))
        eta_o_sib[q] = send(block, block, sib)

    def last_term(q):
        eta_f_sib[q].wait_recv()
        eta_o_sib[q].wait_recv()
        cols = slice(q * quarter, (q + 1) * quarter)
        part = acc[:, cols] - dot(om_left[...], eta_half[:, cols], NN)
        keep = lax.broadcasted_iota(jnp.int32, (1, quarter), 1) + h * half + q * quarter < live
        part = jnp.where(keep, part, 0.0).astype(BF)
        pair_send[q] = part[rows:]
        swaps[q] = send(pair_send.at[q], pair_ref.at[:, eta_cols(q, h)], near)
        pair_ref[:, eta_cols(q, h)] = part[:rows]

    def swapped(q):
        swaps[q].wait_recv()

    plan = [
        (recouple,), (meet,), (own_omega,), (own_left,), (omega_to_far, 1), (recouple_back,), (omega_to_far, 0), (product, 0), (omega_to_far, 3),
        (omega_to_far, 2), (near_omega, 2), (near_omega, 3), (pass_omega, 3), (near_omega, 0), (near_omega, 1), (gather_on, 0), (pass_omega, 1),
        (from_sibling, om_near_sib), (set_weights,), (pass_omega, 0), (product, 1), (weigh, 0), (far_omega, 0), (far_omega, 2), (gather_on, 1),
        (far_omega, 3), (pass_omega, 2), (merge_on, 0), (far_omega, 1), (eta_to_near, 0), (weigh, 1), (eta_to_near, 3), (opposite_omega, 0),
        (eta_to_far, 1), (from_sibling, om_far_sib), (opposite_omega, 3), (opposite_omega, 1), (product, 2), (product, 3), (eta_to_near, 2),
        (eta_to_near, 1), (near_left,), (merge_on, 1), (opposite_omega, 2), (near_eta, 0), (gather_on, 2), (product, 4), (gather_on, 3),
        (first_term, 0), (eta_pass, 0), (eta_pass, 1), (eta_to_far, 0), (gather_on, 4), (weigh, 3), (near_eta, 1), (near_eta, 3), (near_eta, 2),
        (eta_pass, 3), (weigh, 2), (share_near_eta,), (eta_to_far, 3), (weigh, 4), (share_eta, 0), (eta_pass, 2), (finish, 0), (eta_to_far, 2),
        (share_eta, 1), (first_term, rows), (settle_eta,), (last_term, 0), (share_eta, 3), (merge_on, 3), (last_term, 1), (share_eta, 2),
        (merge_on, 4), (merge_on, 2), (last_term, 3), (last_term, 2), (finish, 3), (finish, 1), (finish, 4), (swapped, 1), (swapped, 3), (finish, 2),
        (swapped, 0), (swapped, 2),
    ]
    settled, earlier = 0, {}
    for step, *which in plan:
        upto = settled
        if (step, *which) in ((near_eta, 0), (weigh, 4)):
            upto = earlier.get(step, 0)
        elif step is swapped and "end" not in earlier:
            earlier["end"] = True
            upto = len(started) - 6
        for copy in started[settled:upto]:
            copy.wait_send()
        settled = max(settled, upto)
        if (step, *which) == (product, 2):
            earlier[near_eta] = len(started)
        if (step, *which) == (near_eta, 0):
            earlier[weigh] = len(started)
        step(*which)
    for copy in started[settled:]:
        copy.wait_send()


def body(eta_blocks, omega_blocks, recouple, block_states, cross_map, cross_coef):
    rows, width = eta_blocks.shape[1:]
    half = width // 2
    any_space = pl.BlockSpec(memory_space=pl.ANY)
    smem = pl.BlockSpec(memory_space=pltpu.SMEM)
    square = (2, SIDE, rows, rows)
    out = pltpu.VMEM((rows, width), BF)
    pair_comm, cross_comm = pl.pallas_call(
        kernel,
        out_shape=(out, out),
        in_specs=[smem] * 3 + [any_space] * 3,
        out_specs=(pl.BlockSpec(memory_space=pltpu.VMEM),) * 2,
        scratch_shapes=[
            pltpu.VMEM((width, width), BF),
            pltpu.VMEM((width, half), BF),
            pltpu.VMEM((2 * rows, width), BF),
            pltpu.VMEM((2 * rows, width), BF),
            pltpu.VMEM((rows, width), BF),
            pltpu.VMEM((width, width), BF),
            pltpu.VMEM((rows, width), BF),
            pltpu.VMEM((rows, width), BF),
            pltpu.VMEM((2, SIDE, SIDE, rows, rows), BF),
            pltpu.VMEM(square, F32),
            pltpu.VMEM(square, BF),
            pltpu.VMEM(square, BF),
            pltpu.VMEM(square, BF),
            pltpu.VMEM(square, BF),
            pltpu.VMEM(square, BF),
            pltpu.VMEM(square, BF),
            pltpu.VMEM((2 * rows, half), F32),
            pltpu.VMEM((SIDE, rows, rows), BF),
            pltpu.VMEM((7, 8, 128), F32),
            pltpu.VMEM((32, rows), F32),
            pltpu.SemaphoreType.DMA((COPIES,)),
            pltpu.SemaphoreType.DMA((COPIES,)),
            pltpu.SemaphoreType.DMA((32,)),
            pltpu.SemaphoreType.REGULAR,
            pltpu.SemaphoreType.REGULAR,
        ],
        compiler_params=pltpu.CompilerParams(collective_id=0, has_side_effects=True, vmem_limit_bytes=60 * 1024 * 1024),
        cost_estimate=pl.CostEstimate(flops=10 * rows * width * width, bytes_accessed=14 * rows * width * 2, transcendentals=0),
        name="commutators",
    )(block_states, cross_map, cross_coef, eta_blocks[0], omega_blocks[0], recouple[0])
    return pair_comm[None], cross_comm[None]


def solution(mesh):
    placed = (
        P("chan", "pair", None),
        P("chan", "pair", None),
        P("chan", None, None),
        P("chan"),
        P("chan", None),
        P("chan", None),
    )
    return jax.shard_map(
        body,
        mesh=mesh,
        in_specs=placed,
        out_specs=(P("chan", "pair", None), P("chan", "pair", None)),
        check_vma=False,
    )
```

```python
import functools

import jax
import jax.numpy as jnp
from jax import lax
from jax.experimental import pallas as pl
from jax.experimental.pallas import tpu as pltpu
from jax.sharding import PartitionSpec as P

MESH = pl.DeviceIdType.MESH
BF = jnp.bfloat16
F32 = jnp.float32
NN = (((1,), (0,)), ((), ()))
NT = (((1,), (1,)), ((), ()))
SIDE = 4
PIECES = 4
COPIES = 160


def dot(a, b, dims):
    return lax.dot_general(a, b, dims, preferred_element_type=F32)


def kernel(
    states_ref, map_ref, coef_ref, eta_hbm, omega_hbm, rec_hbm, pair_ref, cross_ref,
    om, eta_half, eta_left, om_left, eta_near, rec, e_ref, f_ref,
    gath, own_sum, sum_next, sum_prev, sum_two, merge, fin_a, fin_b,
    acc, pair_send, wrow, wvec,
    ssem, rsem, lsem, answer, told,
):
    rows, width = eta_hbm.shape
    half = width // 2
    quarter = rows
    sub = rows // PIECES
    ch, pr = lax.axis_index("chan"), lax.axis_index("pair")
    y, z, x, c = ch // SIDE, ch % SIDE, pr // 2, pr % 2
    dn = 1 - 2 * ((x + c) % 2)
    xn, xf, xo = (x + dn + SIDE) % SIDE, (x - dn + SIDE) % SIDE, (x + 2) % SIDE
    turn = 1 - 2 * c
    h = x % 2
    hf = 1 - h
    near, far, sib = (ch, xn * 2 + c), (ch, xf * 2 + c), (ch, x * 2 + (1 - c))

    def along_y(d):
        return (((y + d + SIDE) % SIDE) * SIDE + z, pr)

    def along_z(d):
        return (y * SIDE + (z + d + SIDE) % SIDE, pr)

    moves = (along_z, along_y)
    live = states_ref[0]

    def at(ref, start, size, cols=None):
        start = pl.multiple_of(start, 16)
        if cols is None:
            return ref.at[pl.ds(start, size)]
        return ref.at[pl.ds(start, size), pl.ds(pl.multiple_of(cols[0], 128), cols[1])]

    count = [0, 0]

    def send(src, dst, device):
        i = count[0]
        count[0] += 1
        copy = pltpu.make_async_remote_copy(
            src_ref=src, dst_ref=dst, send_sem=ssem.at[i], recv_sem=rsem.at[i], device_id=device, device_id_type=MESH
        )
        copy.start()
        started.append(copy)
        return copy

    def local(src, dst):
        i = count[1]
        count[1] += 1
        copy = pltpu.make_async_copy(src, dst, lsem.at[i])
        copy.start()
        return copy

    started = []

    barrier = pltpu.get_barrier_semaphore()
    even = (x + c) % 2 == 0
    beside = (near, far, sib)
    across = [move(d) for move in moves for d in (1, -1, 2)]

    def signal(semaphore, device):
        pl.semaphore_signal(semaphore, inc=1, device_id=device, device_id_type=MESH)

    @pl.when(even)
    def _():
        for device in beside:
            signal(barrier, device)

    mine, theirs_n, theirs_f, theirs_o = pr * rows, (xn * 2 + c) * rows, (xf * 2 + c) * rows, (xo * 2 + c) * rows
    get_eta = local(eta_hbm, eta_left.at[pl.ds(0, rows)])
    tile = width // 4
    get_rec = [local(rec_hbm.at[:, pl.ds(t * tile, tile)], rec.at[:, pl.ds(t * tile, tile)]) for t in range(4)]
    get_om = local(omega_hbm, at(om, mine, rows))
    get_half = local(eta_hbm.at[:, pl.ds(pl.multiple_of(h * half, 128), half)], at(eta_half, mine, rows))

    @pl.when(jnp.logical_not(even))
    def _():
        pl.semaphore_wait(barrier, len(beside))
        for device in beside:
            signal(answer, device)

    @pl.when(even)
    def _():
        pl.semaphore_wait(answer, len(beside))

    om_near, om_far = {}, {}

    def omega_to(r, device, kept):
        kept[r] = send(omega_hbm.at[pl.ds(r * sub, sub)], at(om, mine + r * sub, sub), device)

    for r in range(PIECES):
        omega_to(r, near, om_near)
    om_sib = send(omega_hbm, at(om, mine, rows), sib)
    eh_sib = send(eta_hbm.at[:, pl.ds(pl.multiple_of(h * half, 128), half)], at(eta_half, mine, rows), sib)

    lane = lax.broadcasted_iota(jnp.int32, (8, 128), 1)
    weights = jnp.zeros((8, 128), F32)
    for f in range(map_ref.shape[1]):
        weights += jnp.where(lane == map_ref[0, f], coef_ref[0, f], 0.0)
    wrow[0] = weights
    @pl.when(even)
    def _():
        for device in across:
            signal(barrier, device)

    got_w = []

    def meet():
        @pl.when(even)
        def _():
            pl.semaphore_wait(barrier, len(across))
            signal(told, sib)

        @pl.when(jnp.logical_not(even))
        def _():
            pl.semaphore_wait(told, 1)

        for m in range(2):
            for slot, d in ((1, 1), (2, -1), (3, 2)):
                got_w.append(send(wrow.at[0], wrow.at[1 + m * 3 + {1: 2, -1: 1, 2: 3}[d] - 1], moves[m](d)))

    row_no = lax.broadcasted_iota(jnp.int32, (rows, 1), 0)
    col_no = lax.broadcasted_iota(jnp.int32, (1, width), 1)

    def masked(block, first):
        keep = (row_no + first < live) & (col_no < live)
        return jnp.where(keep, block, jnp.zeros((), BF))

    om_on, om_near_sib, om_far_sib, om_opp_sib = {}, {}, {}, {}

    def near_omega(r):
        om_near[r].wait_recv()
        block = at(om, theirs_n + r * sub, sub)
        om_near_sib[r] = send(block, block, sib)

    def omega_to_far(r):
        omega_to(r, far, om_far)

    def far_omega(r):
        om_far[r].wait_recv()
        block = at(om, theirs_f + r * sub, sub)
        om_far_sib[r] = send(block, block, sib)

    def pass_omega(r):
        block = at(om, theirs_n + r * sub, sub)
        om_on[r] = send(block, block, far)

    def opposite_omega(r):
        om_on[r].wait_recv()
        block = at(om, theirs_o + r * sub, sub)
        om_opp_sib[r] = send(block, block, sib)

    def from_sibling(copies):
        for r in range(PIECES):
            copies[r].wait_recv()

    step0 = 1 - 2 * (x % 2)
    chips = [(x, x), ((x + step0 + SIDE) % SIDE, (x - step0 + SIDE) % SIDE), ((x - step0 + SIDE) % SIDE, (x + step0 + SIDE) % SIDE), (xo, xo)]
    parts_of = [(0, 0, rows), (1, 0, rows), (2, 0, rows), (3, 0, rows // 2), (3, rows // 2, rows // 2)]
    quads = {}

    def start_of(p, m):
        k, lo, _ = parts_of[p]
        return pl.multiple_of((chips[k][m] * 2 + m) * rows + lo, 128)

    def cut(ref, p, *index):
        k, lo, size = parts_of[p]
        return ref.at[index[0], k, *index[1:], :, pl.ds(lo, size)]

    def product(p):
        size = parts_of[p][2]
        if p >= 3:
            for r in range((p - 3) * 2, (p - 3) * 2 + 2):
                om_opp_sib[r].wait_recv()
        for m in range(2):
            first = start_of(p, m)
            part = dot(f_ref[...], om[pl.ds(first, size), :], NT)
            keep = lax.broadcasted_iota(jnp.int32, (1, size), 1) + first < live
            cut(gath, p, m, 0)[...] = jnp.where(keep, part, 0.0).astype(BF)
            ahead = send(cut(gath, p, m, 0), cut(gath, p, m, 1), moves[m](turn))
            back = send(cut(gath, p, m, 0), cut(gath, p, m, 2), moves[m](-turn))
            quads[m, p] = [ahead, back]

    def gather_on(p):
        for m in range(2):
            quads[m, p][0].wait_recv()
            quads[m, p].append(send(cut(gath, p, m, 1), cut(gath, p, m, 3), moves[m](turn)))

    def weigh(p):
        for m in range(2):
            quads[m, p][1].wait_recv()
            quads[m, p][2].wait_recv()

            k, lo, size = parts_of[p]
            cols = pl.ds(lo, size)

            def step(i, carry, m=m, k=k, cols=cols, size=size):
                at_rows = pl.ds(pl.multiple_of(i * sub, 16), sub)
                parts = [gath[m, k, s, at_rows, cols].astype(F32) for s in range(4)]
                for t, out in enumerate((own_sum, sum_next, sum_prev, sum_two)):
                    total = sum(wvec[m * 16 + t * 4 + s : m * 16 + t * 4 + s + 1, 0:size] * parts[s] for s in range(4))
                    out[m, k, at_rows, cols] = total.astype(out.dtype)
                return carry

            lax.fori_loop(0, PIECES, step, 0)
            other = moves[1 - m]
            two = send(cut(sum_two, p, m), cut(merge, p, m), other(turn))
            prev = send(cut(sum_prev, p, m), cut(fin_a, p, m), other(-turn))
            quads[m, p] += [two, prev]

    def merge_on(p):
        for m in range(2):
            quads[m, p][3].wait_recv()
            ahead = cut(sum_next, p, m)
            ahead[...] = (ahead[...].astype(F32) + cut(merge, p, m)[...].astype(F32)).astype(BF)
            quads[m, p].append(send(ahead, cut(fin_b, p, m), moves[1 - m](turn)))

    def finish(p):
        for m in range(2):
            quads[m, p][4].wait_recv()
            quads[m, p][5].wait_recv()
            total = cut(own_sum, p, m)[...] + cut(fin_a, p, m)[...].astype(F32) + cut(fin_b, p, m)[...].astype(F32)
            cross_ref[:, pl.ds(start_of(p, m), parts_of[p][2])] = total.astype(BF)

    def recouple():
        get_eta.wait()
        eta_left[0:rows, :] = masked(eta_left[0:rows, :], mine)
        for t in range(4):
            get_rec[t].wait()
            e_ref[:, t * tile : (t + 1) * tile] = dot(eta_left[0:rows, :], rec[:, t * tile : (t + 1) * tile], NN).astype(BF)

    def recouple_back():
        for t in range(4):
            part = dot(e_ref[...], rec[t * tile : (t + 1) * tile, :], NT)
            keep = lax.broadcasted_iota(jnp.int32, (1, tile), 1) + t * tile < live
            f_ref[:, t * tile : (t + 1) * tile] = jnp.where(keep, part, 0.0).astype(BF)

    def own_omega():
        om_sib.wait_recv()
        get_om.wait()

    def set_weights():
        for copy in got_w:
            copy.wait_recv()
        for m in range(2):
            for t, d in enumerate((0, turn, -turn, 2)):
                target = along_y(d)[0] if m == 0 else along_z(d)[0]
                for s in range(4):
                    if s == 0:
                        row = wrow[0]
                    elif s == 3:
                        row = wrow[1 + m * 3 + 2]
                    else:
                        plus, minus = wrow[1 + m * 3], wrow[1 + m * 3 + 1]
                        row = jnp.where((turn if s == 2 else -turn) == 1, plus, minus)
                    value = jnp.sum(jnp.where(lane == target, row, 0.0), axis=1, keepdims=True)[0:1]
                    i = m * 16 + t * 4 + s
                    wvec[i : i + 1, :] = jnp.broadcast_to(value, (1, wvec.shape[1]))

    def own_left():
        om_left[0:rows, :] = masked(om[pl.ds(pl.multiple_of(mine, 16), rows), :], mine)

    def near_left():
        om_left[rows:, :] = masked(om[pl.ds(pl.multiple_of(theirs_n, 16), rows), :], theirs_n)

    eta_n, eta_f, eta_on, eta_f_sib, eta_o_sib, eta_n_sib, own_copy = {}, {}, {}, {}, {}, [], []

    def eta_to_near(r):
        side, first = (h, r) if r < 2 else (hf, r - 2)
        cols = pl.ds(pl.multiple_of(side * half + first * 2 * quarter, 128), 2 * quarter)
        eta_n[r] = send(eta_hbm.at[:, cols], eta_near.at[:, cols], near)

    def eta_cols(q, side):
        return pl.ds(pl.multiple_of(side * half + q * quarter, 128), quarter)

    def eta_to_far(q):
        eta_f[q] = send(eta_hbm.at[:, eta_cols(q, hf)], at(eta_half, mine, rows, (q * quarter, quarter)), far)

    def eta_pass(q):
        eta_on[q] = send(eta_near.at[:, eta_cols(q, hf)], at(eta_half, theirs_n, rows, (q * quarter, quarter)), far)

    half_cols = pl.ds(pl.multiple_of(h * half, 128), half)

    def first_term(lo):
        for t in range(half // 512):
            cols = pl.ds(pl.multiple_of(h * half + t * 512, 128), 512)
            acc[lo : lo + rows, t * 512 : (t + 1) * 512] = dot(eta_left[lo : lo + rows, :], om[:, cols], NN)

    def near_eta(r):
        eta_n[r].wait_recv()

    def share_near_eta():
        eta_n_sib.append(send(eta_near.at[:, half_cols], at(eta_half, theirs_n, rows), sib))
        own_copy.append(local(eta_near.at[:, half_cols], at(eta_half, theirs_n, rows)))
        eta_left[rows:, :] = masked(eta_near[...], theirs_n)

    def settle_eta():
        get_half.wait()
        eh_sib.wait_recv()
        eta_n_sib[0].wait_recv()
        own_copy[0].wait()

    swaps = {}

    def share_eta(q):
        eta_f[q].wait_recv()
        block = at(eta_half, theirs_f, rows, (q * quarter, quarter))
        eta_f_sib[q] = send(block, block, sib)
        eta_on[q].wait_recv()
        block = at(eta_half, theirs_o, rows, (q * quarter, quarter))
        eta_o_sib[q] = send(block, block, sib)

    def last_term(q):
        eta_f_sib[q].wait_recv()
        eta_o_sib[q].wait_recv()
        cols = slice(q * quarter, (q + 1) * quarter)
        part = acc[:, cols] - dot(om_left[...], eta_half[:, cols], NN)
        keep = lax.broadcasted_iota(jnp.int32, (1, quarter), 1) + h * half + q * quarter < live
        part = jnp.where(keep, part, 0.0).astype(BF)
        pair_send[q] = part[rows:]
        swaps[q] = send(pair_send.at[q], pair_ref.at[:, eta_cols(q, h)], near)
        pair_ref[:, eta_cols(q, h)] = part[:rows]

    def swapped(q):
        swaps[q].wait_recv()

    plan = [
        (recouple,), (meet,), (own_omega,), (own_left,), (omega_to_far, 1), (recouple_back,), (omega_to_far, 0), (product, 0), (omega_to_far, 3),
        (omega_to_far, 2), (near_omega, 2), (near_omega, 3), (pass_omega, 3), (near_omega, 0), (near_omega, 1), (gather_on, 0), (pass_omega, 1),
        (from_sibling, om_near_sib), (set_weights,), (pass_omega, 0), (product, 1), (weigh, 0), (far_omega, 0), (far_omega, 2), (gather_on, 1),
        (far_omega, 3), (pass_omega, 2), (merge_on, 0), (far_omega, 1), (eta_to_near, 0), (weigh, 1), (eta_to_near, 3), (opposite_omega, 0),
        (eta_to_far, 1), (from_sibling, om_far_sib), (opposite_omega, 3), (opposite_omega, 1), (product, 2), (product, 3), (eta_to_near, 2),
        (eta_to_near, 1), (near_left,), (merge_on, 1), (opposite_omega, 2), (near_eta, 0), (gather_on, 2), (product, 4), (gather_on, 3),
        (first_term, 0), (eta_pass, 0), (eta_pass, 1), (eta_to_far, 0), (gather_on, 4), (weigh, 3), (near_eta, 1), (near_eta, 3), (near_eta, 2),
        (eta_pass, 3), (weigh, 2), (share_near_eta,), (finish, 1), (eta_to_far, 3), (weigh, 4), (share_eta, 0), (eta_pass, 2), (finish, 0), (eta_to_far, 2),
        (share_eta, 1), (first_term, rows), (settle_eta,), (last_term, 0), (share_eta, 3), (merge_on, 3), (last_term, 1), (share_eta, 2),
        (merge_on, 4), (merge_on, 2), (last_term, 3), (last_term, 2), (finish, 3), (finish, 4), (swapped, 1), (swapped, 3), (finish, 2),
        (swapped, 0), (swapped, 2),
    ]
    settled, earlier = 0, {}
    for step, *which in plan:
        upto = settled
        if (step, *which) in ((near_eta, 0), (weigh, 4)):
            upto = earlier.get(step, 0)
        elif step is swapped and "end" not in earlier:
            earlier["end"] = True
            upto = len(started) - 6
        for copy in started[settled:upto]:
            copy.wait_send()
        settled = max(settled, upto)
        if (step, *which) == (product, 2):
            earlier[near_eta] = len(started)
        if (step, *which) == (near_eta, 0):
            earlier[weigh] = len(started)
        step(*which)
    for copy in started[settled:]:
        copy.wait_send()


def body(eta_blocks, omega_blocks, recouple, block_states, cross_map, cross_coef):
    rows, width = eta_blocks.shape[1:]
    half = width // 2
    any_space = pl.BlockSpec(memory_space=pl.ANY)
    smem = pl.BlockSpec(memory_space=pltpu.SMEM)
    square = (2, SIDE, rows, rows)
    out = pltpu.VMEM((rows, width), BF)
    pair_comm, cross_comm = pl.pallas_call(
        kernel,
        out_shape=(out, out),
        in_specs=[smem] * 3 + [any_space] * 3,
        out_specs=(pl.BlockSpec(memory_space=pltpu.VMEM),) * 2,
        scratch_shapes=[
            pltpu.VMEM((width, width), BF),
            pltpu.VMEM((width, half), BF),
            pltpu.VMEM((2 * rows, width), BF),
            pltpu.VMEM((2 * rows, width), BF),
            pltpu.VMEM((rows, width), BF),
            pltpu.VMEM((width, width), BF),
            pltpu.VMEM((rows, width), BF),
            pltpu.VMEM((rows, width), BF),
            pltpu.VMEM((2, SIDE, SIDE, rows, rows), BF),
            pltpu.VMEM(square, F32),
            pltpu.VMEM(square, BF),
            pltpu.VMEM(square, BF),
            pltpu.VMEM(square, BF),
            pltpu.VMEM(square, BF),
            pltpu.VMEM(square, BF),
            pltpu.VMEM(square, BF),
            pltpu.VMEM((2 * rows, half), F32),
            pltpu.VMEM((SIDE, rows, rows), BF),
            pltpu.VMEM((7, 8, 128), F32),
            pltpu.VMEM((32, rows), F32),
            pltpu.SemaphoreType.DMA((COPIES,)),
            pltpu.SemaphoreType.DMA((COPIES,)),
            pltpu.SemaphoreType.DMA((32,)),
            pltpu.SemaphoreType.REGULAR,
            pltpu.SemaphoreType.REGULAR,
        ],
        compiler_params=pltpu.CompilerParams(collective_id=0, has_side_effects=True, vmem_limit_bytes=60 * 1024 * 1024),
        cost_estimate=pl.CostEstimate(flops=10 * rows * width * width, bytes_accessed=14 * rows * width * 2, transcendentals=0),
        name="commutators",
    )(block_states, cross_map, cross_coef, eta_blocks[0], omega_blocks[0], recouple[0])
    return pair_comm[None], cross_comm[None]


def solution(mesh):
    placed = (
        P("chan", "pair", None),
        P("chan", "pair", None),
        P("chan", None, None),
        P("chan"),
        P("chan", None),
        P("chan", None),
    )
    return jax.shard_map(
        body,
        mesh=mesh,
        in_specs=placed,
        out_specs=(P("chan", "pair", None), P("chan", "pair", None)),
        check_vma=False,
    )
```
